128 devices in a mesh: ctx: 16 (over x, y), head: 8 (over z, core).
Axes of the slice: x: 4, y: 4, z: 4, core: 2. Of those that a mesh axis runs over, the one named last changes fastest.
Arguments:
- q_rows: bfloat16 [16384, 8192], P(('ctx', 'head')), may hold values from -75 to 75
- key_rows: bfloat16 [16384, 1024], P('ctx', 'head'), may hold values from -6 to 6
- value_rows: bfloat16 [16384, 1024], P('ctx', 'head'), may hold values from -6 to 6
- doc_lengths: int32 [16], replicated, may hold values from 1 to 9216, 16384 in all
- window_widths: int32 [8], replicated, may hold values from 512 to 2048, as said below
- sink_widths: int32 [8], replicated, may hold values from 16 to 32, as said below
Outputs:
- attended: bfloat16 [16384, 8192], P('ctx', 'head')
The draws below stay inside these ranges and needn't reach their ends.
Inputs may be any that keep to these rules, and one draw needn't show every extreme that they name: `doc_lengths`: each is at least 1; they sum to 16384; the longest equals 9216. `window_widths`: at least one KV head has a window of exactly 2048. `sink_widths`: at least one KV head has exactly 32 sink tokens.
All inputs are finite; a program needn't handle non-finite values.
Results may differ from the reference program's by a relative error of at most 0.004.
Values may be sent and summed in bfloat16 or wider, within the bound.
A program may use at most 128 MiB of HBM per device.

```python
import math
import jax
import jax.numpy as jnp
import numpy as np
from jax import lax

HD = 128
QPG = 8
KV_HEADS = 8
Q_HEADS = 64
TOK_DEV = 1024
WSPAN = 2
SINK_MAX = 32
TOKENS = 16384
DOCS = 16


def draw_q_rows(key, part):
    key = jax.random.fold_in(key, 11)
    drawn = jnp.clip(jax.random.normal(key, (TOKENS, Q_HEADS * HD), jnp.float32), -6.0, 6.0)
    return drawn.astype(jnp.bfloat16)


def draw_key_rows(key, part):
    key = jax.random.fold_in(key, 23)
    drawn = jnp.clip(jax.random.normal(key, (TOKENS, KV_HEADS * HD), jnp.float32), -6.0, 6.0)
    return drawn.astype(jnp.bfloat16)


def draw_window_widths(key, part):
    key = jax.random.fold_in(key, 31)
    first, second = jax.random.split(key)
    widths = jax.random.randint(first, (KV_HEADS,), TOK_DEV // 2, WSPAN * TOK_DEV + 1)
    chosen = jax.random.randint(second, (), 0, KV_HEADS)
    return widths.at[chosen].set(WSPAN * TOK_DEV).astype(jnp.int32)


def draw_sink_widths(key, part):
    key = jax.random.fold_in(key, 47)
    first, second = jax.random.split(key)
    widths = jax.random.randint(first, (KV_HEADS,), max(SINK_MAX // 2, 1), SINK_MAX + 1)
    chosen = jax.random.randint(second, (), 0, KV_HEADS)
    return widths.at[chosen].set(SINK_MAX).astype(jnp.int32)


def block_scale(rng, extent, shards, low, top_value):
    def one(dim, parts):
        draws = jax.random.uniform(jax.random.fold_in(jax.random.fold_in(rng, 6), dim), (parts,), jnp.float32, low / len(shards), top_value / len(shards))
        return jnp.repeat(jnp.exp(draws), extent[dim] // parts).reshape((-1,) + (1,) * (len(extent) - dim - 1))

    gain = one(*shards[0])
    for cut in shards[1:]:
        gain = gain * one(*cut)
    return gain


def length_profile(count, total, most, skew):
    portions = [(1 << 20) // math.isqrt(rank ** skew) + 1 for rank in range(2, count + 1)]
    surplus, holding = total - most - (count - 1), [1] * (count - 1)
    while surplus > 0:
        candidates = [i for i in range(count - 1) if holding[i] < most]
        pool, budget = sum([portions[i] for i in candidates]), surplus
        for i in candidates:
            more = min(most - holding[i], max(1, budget * portions[i] // pool), surplus)
            holding[i] = holding[i] + more
            surplus = surplus - more
    return np.array([most] + holding)


def uneven_parts(own_key, amount, total, most, slope):
    if amount == 2:
        one = jax.random.randint(own_key, (), max(1, total - most), min(most, total - 1) + 1)
        return jnp.stack([one, total - one])
    tallies = jnp.asarray(length_profile(amount, total, most, slope), jnp.int32)
    twos = (amount - 1) // 2
    donor, receiver = tallies[1:1 + 2 * twos:2], tallies[2:2 + 2 * twos:2]
    margin = jnp.minimum(donor - 1, most - receiver)
    moved = jax.random.randint(jax.random.fold_in(own_key, 1), (twos,), 0, 1 << 20) % (margin + 1)
    tallies = tallies.at[1:1 + 2 * twos:2].set(donor - moved).at[2:2 + 2 * twos:2].set(receiver + moved)
    return tallies[jax.random.permutation(jax.random.fold_in(own_key, 2), amount)]


def bell_draw(own_key, dims, scale, bound, cuts=(), kind=jnp.bfloat16):
    entries = jax.random.normal(own_key, dims, jnp.float32) * scale
    if len(cuts) > 0:
        entries = block_scale(own_key, dims, cuts, -0.22, 0.18) * entries
    return jnp.clip(entries, min=-bound, max=bound).astype(kind)


def setup_inputs(seed: int = 0) -> dict:
    splits = jax.random.split(jax.random.key(seed), 7)
    q_rows = draw_q_rows(jax.random.fold_in(splits[6], 71), 0)
    key_rows = draw_key_rows(jax.random.fold_in(splits[6], 71), 0)
    value_rows = bell_draw(splits[2], (TOKENS, KV_HEADS * HD), 1.0, 6.0, ((0, 16), (1, 8)))
    doc_lengths = uneven_parts(splits[3], DOCS, TOKENS, TOKENS // 2 + TOK_DEV, 2).astype(jnp.int32)
    window_widths = draw_window_widths(jax.random.fold_in(splits[6], 71), 0)
    sink_widths = draw_sink_widths(jax.random.fold_in(splits[6], 71), 0)
    return {"q_rows": q_rows, "key_rows": key_rows, "value_rows": value_rows, "doc_lengths": doc_lengths, "window_widths": window_widths, "sink_widths": sink_widths}


def doc_index(positions, starts):
    return jnp.sum((positions[:, None] >= starts[None, :]).astype(jnp.int32), axis=1) - 1


def reference(q_rows, key_rows, value_rows, doc_lengths, window_widths, sink_widths):
    starts = (jnp.cumsum(doc_lengths) - doc_lengths).astype(jnp.int32)
    span = WSPAN * TOK_DEV
    block = math.gcd(256, TOKENS)
    offsets = jnp.arange(SINK_MAX, dtype=jnp.int32)
    sink_pos = (starts[:, None] + offsets[None, :]).reshape(-1)
    sink_rank = jnp.tile(offsets, DOCS)
    sink_doc = jnp.repeat(jnp.arange(DOCS, dtype=jnp.int32), SINK_MAX)
    sink_live = sink_rank < jnp.repeat(doc_lengths, SINK_MAX)
    clipped = jnp.clip(sink_pos, 0, TOKENS - 1).astype(jnp.int32)
    sink_keys = jnp.take(key_rows, clipped, axis=0)
    sink_values = jnp.take(value_rows, clipped, axis=0)
    padding = jnp.zeros((span, KV_HEADS * HD), jnp.bfloat16)
    padded_keys = jnp.concatenate([padding, key_rows], axis=0)
    padded_values = jnp.concatenate([padding, value_rows], axis=0)
    all_docs = doc_index(jnp.arange(TOKENS, dtype=jnp.int32), starts)
    score_scale = HD ** -0.5

    def attend(index):
        first = (index * block).astype(jnp.int32)
        query_pos = first + jnp.arange(block, dtype=jnp.int32)
        query_doc = lax.dynamic_slice_in_dim(all_docs, first, block)
        queries = lax.dynamic_slice_in_dim(q_rows, first, block, 0).astype(jnp.float32).reshape(block, KV_HEADS, QPG, HD)
        near_keys = lax.dynamic_slice_in_dim(padded_keys, first, span + block, 0)
        near_values = lax.dynamic_slice_in_dim(padded_values, first, span + block, 0)
        near_pos = first - span + jnp.arange(span + block, dtype=jnp.int32)
        near_doc = doc_index(near_pos, starts)
        cand_keys = jnp.concatenate([near_keys, sink_keys], axis=0).astype(jnp.float32).reshape(-1, KV_HEADS, HD)
        cand_values = jnp.concatenate([near_values, sink_values], axis=0).astype(jnp.float32).reshape(-1, KV_HEADS, HD)
        gap_near = query_pos[:, None] - near_pos[None, :]
        near_ok = (near_doc[None, :] == query_doc[:, None]) & (gap_near >= 0) & (near_pos[None, :] >= 0)
        near_mask = near_ok[None] & (gap_near[None] < window_widths[:, None, None])
        gap_sink = query_pos[:, None] - sink_pos[None, :]
        sink_ok = sink_live[None, :] & (sink_doc[None, :] == query_doc[:, None]) & (gap_sink >= 0)
        sink_mask = sink_ok[None] & (gap_sink[None] >= window_widths[:, None, None]) & (sink_rank[None, None, :] < sink_widths[:, None, None])
        mask = jnp.concatenate([near_mask, sink_mask], axis=2)[:, None]
        scores = jnp.einsum("qgjd,kgd->gjqk", queries, cand_keys) * score_scale
        top = jnp.max(jnp.where(mask, scores, -jnp.inf), axis=-1, keepdims=True)
        raw = jnp.where(mask, jnp.exp(scores - top), 0.0)
        total = jnp.sum(raw, axis=-1)
        weights = lax.optimization_barrier(raw.astype(jnp.bfloat16)).astype(jnp.float32)
        summed = jnp.einsum("gjqk,kgd->qgjd", weights, cand_values)
        result = summed / jnp.transpose(total, (2, 0, 1))[..., None]
        return result.reshape(block, Q_HEADS * HD).astype(jnp.bfloat16)

    pieces = lax.map(attend, jnp.arange(TOKENS // block, dtype=jnp.int32))
    return pieces.reshape(TOKENS, Q_HEADS * HD)
```

```python
import functools

import jax
import jax.numpy as jnp
from jax import lax
from jax.experimental import pallas as pl
from jax.experimental.pallas import tpu as pltpu
from jax.sharding import PartitionSpec as P

HD = 128
QPG = 8
WSPAN = 2
SINK_MAX = 32
MESH = pl.DeviceIdType.MESH
EXP2_SCALE = HD ** (-0.5) * 1.4426950408889634
NT = (((1,), (1,)), ((), ()))
HIDDEN = -1e30


def kernel(
    ctx_n, head_n, docs,
    lengths, windows, sinks, q_hbm, k_hbm, v_hbm, out_hbm,
    qbuf, kbuf, vbuf, obuf, bias, ident, first_of, sink_k, sink_v, sink_own, sink_in1, sink_mid, sink_in2,
    q_local, kv_local, q_send, q_recv, kv_send, kv_recv, s1_send, s1_recv, s2_send, s2_recv, o_sem,
):
    ctx = lax.axis_index("ctx")
    head = lax.axis_index("head")
    rows = k_hbm.shape[0]
    chunk = q_hbm.shape[0]
    width = QPG * HD
    near = WSPAN * rows
    reach = near + chunk
    z, core, zn = head // 2, head % 2, head_n // 2
    base = ctx * rows

    def back(d):
        return lax.rem(ctx + d + ctx_n, ctx_n)

    step1 = (1, 2, 3)
    step2 = (1, 5, 9, 13)
    order = [(dz, dc) for dz, dc in ((0, 1), (1, 0), (3, 0), (1, 1), (3, 1), (2, 0), (2, 1))]

    def peer(dz, dc):
        return lax.rem(z + dz, zn) * 2 + lax.rem(core + dc, 2)

    barrier = pltpu.get_barrier_semaphore()
    for d in (13, 9, 5, 3, 2, 1):
        pl.semaphore_signal(barrier, inc=1, device_id=(back(-d), head), device_id_type=MESH)
    for dz, dc in order:
        pl.semaphore_signal(barrier, inc=1, device_id=(ctx, peer(dz, dc)), device_id_type=MESH)

    own_q = pltpu.make_async_copy(
        q_hbm.at[:, pl.ds(pl.multiple_of(head * width, width), width)], qbuf.at[head], q_local
    )
    own_k = pltpu.make_async_copy(k_hbm, kbuf.at[pl.ds(near, rows)], kv_local.at[0])
    own_v = pltpu.make_async_copy(v_hbm, vbuf.at[pl.ds(near, rows)], kv_local.at[1])
    own_k.start()
    own_v.start()
    own_q.start()

    starts = []
    running = jnp.int32(0)
    for d in range(docs):
        starts.append(running)
        running = running + lengths[d]

    def start_of(position):
        found = jnp.int32(-1)
        for s in starts:
            found = jnp.where(position >= s, s, found)
        return found

    window = windows[head]
    sink_width = sinks[head]
    last_doc = {d: start_of(base - d * rows + rows - 1) for d in (0, 1, 2, 3, 5, 9, 13)}
    doc_a = start_of(base)
    doc_b = start_of(base + rows // 2 - 1)
    doc_b = jnp.where(doc_b > base, doc_b, -1)

    iota_r = lax.broadcasted_iota(jnp.int32, (chunk, HD), 0)
    iota_c = lax.broadcasted_iota(jnp.int32, (chunk, HD), 1)
    ident[...] = jnp.where(iota_r == iota_c, 1.0, 0.0).astype(jnp.bfloat16)
    grid_pos = base + lax.broadcasted_iota(jnp.int32, (rows // HD, HD), 0) * HD + lax.broadcasted_iota(
        jnp.int32, (rows // HD, HD), 1
    )
    found = jnp.zeros((rows // HD, HD), jnp.int32)
    for s in starts:
        found = jnp.where(grid_pos >= s, s, found)
    first_of[...] = found
    sink_k[...] = jnp.zeros_like(sink_k)
    sink_v[...] = jnp.zeros_like(sink_v)

    pl.semaphore_wait(barrier, len(order) + 6)

    def q_copy(target, source):
        return pltpu.make_async_remote_copy(
            src_ref=q_hbm.at[:, pl.ds(pl.multiple_of(target * width, width), width)],
            dst_ref=qbuf.at[source],
            send_sem=q_send.at[target],
            recv_sem=q_recv.at[source],
            device_id=(ctx, target),
            device_id_type=MESH,
        )

    def kv_copy(d, which):
        src = (k_hbm, v_hbm)[which]
        dst = (kbuf, vbuf)[which]
        return pltpu.make_async_remote_copy(
            src_ref=src,
            dst_ref=dst.at[pl.ds(near - d * rows, rows)],
            send_sem=kv_send.at[d - 1, which],
            recv_sem=kv_recv.at[d - 1, which],
            device_id=(back(d), head),
            device_id_type=MESH,
        )

    for which in (0, 1):
        kv_copy(1, which).start()
    for dz, dc in order:
        q_copy(peer(dz, dc), head).start()
    for which in (0, 1):
        kv_copy(2, which).start()

    own_k.wait()
    own_v.wait()
    at = base + lax.broadcasted_iota(jnp.int32, (SINK_MAX, rows), 1)
    rank = lax.broadcasted_iota(jnp.int32, (SINK_MAX, rows), 0)
    pick = jnp.concatenate(
        [jnp.where(at == s + rank, 1.0, 0.0).astype(jnp.bfloat16) for s in (last_doc[0], doc_a, doc_b)], axis=0
    )
    own = jnp.concatenate([kbuf[pl.ds(near, rows), :], vbuf[pl.ds(near, rows), :]], axis=1)
    picked = jnp.dot(pick, own, preferred_element_type=jnp.float32).astype(jnp.bfloat16)
    n = SINK_MAX
    sink_own[pl.ds(0, n), :] = picked[:n, :HD]
    sink_own[pl.ds(n, n), :] = picked[:n, HD:]
    sink_k[pl.ds(0, n), :] = picked[n : 2 * n, :HD]
    sink_v[pl.ds(0, n), :] = picked[n : 2 * n, HD:]
    sink_k[pl.ds(n, n), :] = picked[2 * n : 3 * n, :HD]
    sink_v[pl.ds(n, n), :] = picked[2 * n : 3 * n, HD:]

    def s1_copy(j):
        return pltpu.make_async_remote_copy(
            src_ref=sink_own, dst_ref=sink_in1.at[j], send_sem=s1_send.at[j], recv_sem=s1_recv.at[j],
            device_id=(back(step1[j]), head), device_id_type=MESH,
        )

    def s2_copy(j):
        return pltpu.make_async_remote_copy(
            src_ref=sink_mid, dst_ref=sink_in2.at[j], send_sem=s2_send.at[j], recv_sem=s2_recv.at[j],
            device_id=(back(step2[j]), head), device_id_type=MESH,
        )

    for j in range(len(step1)):
        s1_copy(j).start()
    same = lambda a, b: jnp.full((2 * n, HD), a, jnp.int32) == jnp.full((2 * n, HD), b, jnp.int32)
    for j in range(len(step1)):
        s1_copy(j).wait()
    mid = sink_own[...].astype(jnp.float32)
    for j, d in enumerate(step1):
        mid = mid + jnp.where(same(last_doc[d], last_doc[0]), sink_in1[j].astype(jnp.float32), 0.0)
    sink_mid[...] = mid.astype(jnp.bfloat16)
    for j in range(len(step2)):
        s2_copy(j).start()
    for j in range(len(step2)):
        s2_copy(j).wait()
    got = jnp.zeros((2 * n, HD), jnp.float32)
    for j, d in enumerate(step2):
        got = got + jnp.where(same(last_doc[d], doc_a), sink_in2[j].astype(jnp.float32), 0.0)
    sink_k[pl.ds(0, n), :] = (sink_k[pl.ds(0, n), :].astype(jnp.float32) + got[:n]).astype(jnp.bfloat16)
    sink_v[pl.ds(0, n), :] = (sink_v[pl.ds(0, n), :].astype(jnp.float32) + got[n:]).astype(jnp.bfloat16)

    for d in (1, 2):
        for which in (0, 1):
            kv_copy(d, which).wait()
    own_q.wait()

    srank = lax.broadcasted_iota(jnp.int32, (HD, chunk), 0)

    def one_chunk(s, carry):
        dz = jnp.where(s < 2, 0, jnp.where(s < 6, 1 + 2 * (s % 2), 2))
        dc = jnp.where(s < 2, s, jnp.where(s < 6, s // 2 - 1, s - 6))
        i = peer(dz, dc)

        @pl.when(s > 0)
        def _():
            q_copy(i, i).wait()

        lo_row = pl.multiple_of(i * chunk, chunk)
        t = base + i * chunk + lax.broadcasted_iota(jnp.int32, (1, chunk), 1)
        first = first_of[pl.ds(i, 1), :]
        low = jnp.maximum(first, t - window + 1)
        kp = base - near + i * chunk + lax.broadcasted_iota(jnp.int32, (reach, chunk), 0)
        bias[pl.ds(0, reach), :] = jnp.where((kp <= t) & (kp >= low), 0.0, HIDDEN).astype(jnp.bfloat16)
        doc = jnp.where(srank < n, doc_a, jnp.where(srank < 2 * n, doc_b, -1))
        r = srank % n
        seen = (r < sink_width) & (doc == first) & (doc + r <= t - window)
        bias[pl.ds(reach, HD), :] = jnp.where(seen, 0.0, HIDDEN).astype(jnp.bfloat16)

        keys = jnp.concatenate([kbuf[pl.ds(lo_row, reach), :], sink_k[...]], axis=0)
        vals = jnp.concatenate([vbuf[pl.ds(lo_row, reach), :], sink_v[...]], axis=0)
        keys = jnp.concatenate([keys, bias[...]], axis=1)
        vals = jnp.concatenate([vals, jnp.ones((reach + HD, HD), jnp.bfloat16)], axis=1)
        unit = ident[...]
        for h in range(0, QPG, 2):
            left = jnp.concatenate(
                [jnp.concatenate([qbuf[i, :, a * HD : (a + 1) * HD], unit], axis=1) for a in (h, h + 1)], axis=0
            )
            scores = lax.dot_general(left, keys, NT, preferred_element_type=jnp.float32)
            top = jnp.max(scores, axis=1, keepdims=True)
            raw = jnp.exp2(scores * EXP2_SCALE - top * EXP2_SCALE).astype(jnp.bfloat16)
            summed = jnp.dot(raw, vals, preferred_element_type=jnp.float32)
            result = (summed[:, :HD] / summed[:, HD:]).astype(jnp.bfloat16)
            for a in (0, 1):
                obuf[pl.ds(lo_row, chunk), (h + a) * HD : (h + a + 1) * HD] = result[a * chunk : (a + 1) * chunk]
        return carry

    lax.fori_loop(0, head_n, one_chunk, 0)
    result_copy = pltpu.make_async_copy(obuf, out_hbm, o_sem)
    result_copy.start()
    result_copy.wait()


def per_device(ctx_n, head_n, q_rows, key_rows, value_rows, doc_lengths, window_widths, sink_widths):
    rows = key_rows.shape[0]
    chunk = q_rows.shape[0]
    docs = doc_lengths.shape[0]
    span = (WSPAN + 1) * rows
    bf = jnp.bfloat16
    n = SINK_MAX
    dma = pltpu.SemaphoreType.DMA
    return pl.pallas_call(
        functools.partial(kernel, ctx_n, head_n, docs),
        out_shape=jax.ShapeDtypeStruct((rows, QPG * HD), bf),
        in_specs=[pl.BlockSpec(memory_space=pltpu.SMEM)] * 3 + [pl.BlockSpec(memory_space=pl.ANY)] * 3,
        out_specs=pl.BlockSpec(memory_space=pl.ANY),
        scratch_shapes=[
            pltpu.VMEM((head_n, chunk, QPG * HD), bf),
            pltpu.VMEM((span, HD), bf),
            pltpu.VMEM((span, HD), bf),
            pltpu.VMEM((rows, QPG * HD), bf),
            pltpu.VMEM((WSPAN * rows + chunk + HD, chunk), bf),
            pltpu.VMEM((chunk, HD), bf),
            pltpu.VMEM((rows // HD, HD), jnp.int32),
            pltpu.VMEM((HD, HD), bf),
            pltpu.VMEM((HD, HD), bf),
            pltpu.VMEM((2 * n, HD), bf),
            pltpu.VMEM((3, 2 * n, HD), bf),
            pltpu.VMEM((2 * n, HD), bf),
            pltpu.VMEM((4, 2 * n, HD), bf),
            dma,
            dma((2,)),
            dma((head_n,)),
            dma((head_n,)),
            dma((2, 2)),
            dma((2, 2)),
            dma((3,)),
            dma((3,)),
            dma((4,)),
            dma((4,)),
            dma,
        ],
        compiler_params=pltpu.CompilerParams(
            collective_id=0, has_side_effects=True, vmem_limit_bytes=48 * 2**20
        ),
        cost_estimate=pl.CostEstimate(
            flops=4 * rows * QPG * HD * (WSPAN * rows + 2 * chunk),
            bytes_accessed=2 * (2 * rows * QPG * HD + 2 * rows * HD),
            transcendentals=rows * QPG * (WSPAN * rows + 2 * chunk),
        ),
        name="attention",
    )(doc_lengths, window_widths, sink_widths, q_rows, key_rows, value_rows)


def solution(mesh):
    in_specs = (P(("ctx", "head"), None), P("ctx", "head"), P("ctx", "head"), P(), P(), P())
    out_specs = P("ctx", "head")
    return jax.shard_map(
        functools.partial(per_device, mesh.shape["ctx"], mesh.shape["head"]),
        mesh=mesh, in_specs=in_specs, out_specs=out_specs, check_vma=False,
    )
```

```python
import functools

import jax
import jax.numpy as jnp
from jax import lax
from jax.experimental import pallas as pl
from jax.experimental.pallas import tpu as pltpu
from jax.sharding import PartitionSpec as P

HD = 128
QPG = 8
WSPAN = 2
SINK_MAX = 32
MESH = pl.DeviceIdType.MESH
EXP2_SCALE = HD ** (-0.5) * 1.4426950408889634
NT = (((1,), (1,)), ((), ()))
HIDDEN = -1e30


def kernel(
    ctx_n, head_n, docs,
    lengths_hbm, windows_hbm, sinks_hbm, q_hbm, k_hbm, v_hbm, out_hbm,
    qbuf, kbuf, vbuf, obuf, held, bias, ident, first_of, sink_k, sink_v, sink_own, sink_in1, sink_mid, sink_in2,
    relay, acc, tops, lengths, windows, sinks,
    small_local, q_local, kv_local, q_send, q_recv, kv_send, kv_recv, relay_send, relay_recv,
    s1_send, s1_recv, s2_send, s2_recv, o_sem,
):
    ctx = lax.axis_index("ctx")
    head = lax.axis_index("head")
    rows = k_hbm.shape[0]
    chunk = q_hbm.shape[0]
    width = QPG * HD
    near = WSPAN * rows
    z, core, zn = head // 2, head % 2, head_n // 2
    base = ctx * rows

    def back_of(c):
        return lax.rem(c + ctx_n, ctx_n)

    def back(d):
        return back_of(ctx + d)

    step1 = (1, 2, 3)
    step2 = (1, 5, 9, 13)
    order = [(dz, dc) for dz, dc in ((0, 1), (1, 0), (3, 0), (1, 1), (3, 1), (2, 0), (2, 1))]

    y_n = 4
    x, y = ctx // y_n, ctx % y_n
    below = x * y_n + lax.rem(y + y_n - 1, y_n)
    above = x * y_n + lax.rem(y + 1, y_n)
    relay_to = back_of(above + 2)
    two_back = back_of(ctx - 2)
    relay_from = two_back // y_n * y_n + lax.rem(two_back + y_n - 1, y_n)

    def peer(dz, dc):
        return lax.rem(z + dz, zn) * 2 + lax.rem(core + dc, 2)

    barrier = pltpu.get_barrier_semaphore()
    for d in (13, 9, 5, 3, 2, 1):
        pl.semaphore_signal(barrier, inc=1, device_id=(back(-d), head), device_id_type=MESH)
    for c in (relay_from, above):
        pl.semaphore_signal(barrier, inc=1, device_id=(c, head), device_id_type=MESH)
    for dz, dc in order:
        pl.semaphore_signal(barrier, inc=1, device_id=(ctx, peer(dz, dc)), device_id_type=MESH)

    own_q = pltpu.make_async_copy(
        q_hbm.at[:, pl.ds(pl.multiple_of(head * width, width), width)], qbuf.at[head], q_local
    )
    own_k = pltpu.make_async_copy(k_hbm, kbuf.at[pl.ds(near, rows)], kv_local.at[0])
    own_v = pltpu.make_async_copy(v_hbm, vbuf.at[pl.ds(near, rows)], kv_local.at[1])
    small = [
        pltpu.make_async_copy(src, dst, small_local.at[j])
        for j, (src, dst) in enumerate(((lengths_hbm, lengths), (windows_hbm, windows), (sinks_hbm, sinks)))
    ]
    for copy in small:
        copy.start()
    own_k.start()
    own_v.start()
    own_q.start()
    for copy in small:
        copy.wait()

    starts = []
    running = jnp.int32(0)
    for d in range(docs):
        starts.append(running)
        running = running + lengths[d]

    def start_of(position):
        found = jnp.int32(-1)
        for s in starts:
            found = jnp.where(position >= s, s, found)
        return found

    window = windows[head]
    sink_width = sinks[head]
    last_doc = {d: start_of(base - d * rows + rows - 1) for d in (0, 1, 2, 3, 5, 9, 13)}
    doc_a = start_of(base)
    doc_b = start_of(base + rows // 2 - 1)
    doc_b = jnp.where(doc_b > base, doc_b, -1)

    iota_r = lax.broadcasted_iota(jnp.int32, (chunk, HD), 0)
    iota_c = lax.broadcasted_iota(jnp.int32, (chunk, HD), 1)
    ident[...] = jnp.where(iota_r == iota_c, 1.0, 0.0).astype(jnp.bfloat16)
    grid_pos = base + lax.broadcasted_iota(jnp.int32, (rows // HD, HD), 0) * HD + lax.broadcasted_iota(
        jnp.int32, (rows // HD, HD), 1
    )
    found = jnp.zeros((rows // HD, HD), jnp.int32)
    for s in starts:
        found = jnp.where(grid_pos >= s, s, found)
    first_of[...] = found
    sink_k[...] = jnp.zeros_like(sink_k)
    sink_v[...] = jnp.zeros_like(sink_v)

    n = SINK_MAX
    srank = lax.broadcasted_iota(jnp.int32, (HD, chunk), 0)

    def place(s):
        dz = jnp.where(s < 2, 0, jnp.where(s < 6, 1 + 2 * (s % 2), 2))
        dc = jnp.where(s < 2, s, jnp.where(s < 6, s // 2 - 1, s - 6))
        return peer(dz, dc)

    def limits(i):
        t = base + i * chunk + lax.broadcasted_iota(jnp.int32, (1, chunk), 1)
        first = first_of[pl.ds(i, 1), :]
        return t, first, jnp.maximum(first, t - window + 1)

    def set_sink_bias(slot, at, t, first):
        doc = jnp.where(srank < n, doc_a, jnp.where(srank < 2 * n, doc_b, -1))
        r = srank % n
        seen = (r < sink_width) & (doc == first) & (doc + r <= t - window)
        bias[slot, pl.ds(at, HD), :] = jnp.where(seen, 0.0, HIDDEN).astype(jnp.bfloat16)

    def pipeline(lo, hi, reach, row_of, with_sinks, stage, wait_queries):
        total = reach + (HD if with_sinks else 0)

        def set_bias(i, slot):
            t, first, low = limits(i)
            kp = base - near + row_of(i) + lax.broadcasted_iota(jnp.int32, (reach, chunk), 0)
            bias[slot, pl.ds(0, reach), :] = jnp.where((kp <= t) & (kp >= low), 0.0, HIDDEN).astype(jnp.bfloat16)
            if with_sinks:
                set_sink_bias(slot, reach, t, first)

        def score(i, slot, h):
            keys = kbuf[pl.ds(row_of(i), reach), :]
            if with_sinks:
                keys = jnp.concatenate([keys, sink_k[...]], axis=0)
            keys = jnp.concatenate([keys, bias[slot, pl.ds(0, total), :]], axis=1)
            unit = ident[...]
            left = jnp.concatenate(
                [jnp.concatenate([qbuf[i, :, a * HD : (a + 1) * HD], unit], axis=1) for a in (h, h + 1)], axis=0
            )
            return lax.dot_general(left, keys, NT, preferred_element_type=jnp.float32)

        def finish(s, i, h, scores):
            vals = vbuf[pl.ds(row_of(i), reach), :]
            if with_sinks:
                vals = jnp.concatenate([vals, sink_v[...]], axis=0)
            vals = jnp.concatenate([vals, jnp.ones((total, HD), jnp.bfloat16)], axis=1)
            span = pl.ds(h * chunk, 2 * chunk)
            top = jnp.max(scores, axis=1, keepdims=True)
            if stage == "last":
                old = tops[s, span, :]
                top = jnp.maximum(old[:, :1], top)
            raw = jnp.exp2(scores * EXP2_SCALE - top * EXP2_SCALE).astype(jnp.bfloat16)
            summed = jnp.dot(raw, vals, preferred_element_type=jnp.float32)
            if stage == "first":
                tops[s, span, :] = jnp.broadcast_to(top, (2 * chunk, HD))
                acc[s, span, :] = summed
                return
            if stage == "last":
                factor = jnp.exp2(old * EXP2_SCALE - jnp.broadcast_to(top * EXP2_SCALE, (2 * chunk, HD)))
                summed = summed + acc[s, span, :] * jnp.concatenate([factor, factor], axis=1)
            result = (summed[:, :HD] / summed[:, HD:]).astype(jnp.bfloat16)
            for a in (0, 1):
                obuf[pl.ds(pl.multiple_of(i * chunk, chunk), chunk), (h + a) * HD : (h + a + 1) * HD] = result[
                    a * chunk : (a + 1) * chunk
                ]

        def body(s, carry):
            slot = lax.rem(s - lo, 2)
            later = jnp.where(s + 1 < hi, s + 1, s)
            i, j = place(s), place(later)
            if wait_queries:

                @pl.when(s + 1 < hi)
                def _():
                    q_copy(j, j).wait()

            set_bias(j, 1 - slot)
            scores = held[:, pl.ds(0, total)]
            for h in range(0, QPG, 2):
                ahead = score(i, slot, h + 2) if h + 2 < QPG else score(j, 1 - slot, 0)
                finish(s, i, h, scores)
                scores = ahead
            held[:, pl.ds(0, total)] = scores
            if stage != "first":
                o_copy(i).start()
            return carry

        i = place(lo)
        if wait_queries and lo > 0:
            q_copy(i, i).wait()
        set_bias(i, 0)
        held[:, pl.ds(0, total)] = score(i, 0, 0)
        lax.fori_loop(lo, hi, body, 0)

    def o_copy(i):
        span = pl.ds(pl.multiple_of(i * chunk, chunk), chunk)
        return pltpu.make_async_copy(obuf.at[span], out_hbm.at[span], o_sem.at[i])

    own_k.wait()
    own_v.wait()
    at = base + lax.broadcasted_iota(jnp.int32, (SINK_MAX, rows), 1)
    rank = lax.broadcasted_iota(jnp.int32, (SINK_MAX, rows), 0)
    pick = jnp.concatenate(
        [jnp.where(at == s + rank, 1.0, 0.0).astype(jnp.bfloat16) for s in (last_doc[0], doc_a, doc_b)], axis=0
    )
    own = jnp.concatenate([kbuf[pl.ds(near, rows), :], vbuf[pl.ds(near, rows), :]], axis=1)
    picked = jnp.dot(pick, own, preferred_element_type=jnp.float32).astype(jnp.bfloat16)
    sink_own[pl.ds(0, n), :] = picked[:n, :HD]
    sink_own[pl.ds(n, n), :] = picked[:n, HD:]
    sink_k[pl.ds(0, n), :] = picked[n : 2 * n, :HD]
    sink_v[pl.ds(0, n), :] = picked[n : 2 * n, HD:]
    sink_k[pl.ds(n, n), :] = picked[2 * n : 3 * n, :HD]
    sink_v[pl.ds(n, n), :] = picked[2 * n : 3 * n, HD:]

    pl.semaphore_wait(barrier, len(order) + 8)

    def q_copy(target, source):
        return pltpu.make_async_remote_copy(
            src_ref=q_hbm.at[:, pl.ds(pl.multiple_of(target * width, width), width)],
            dst_ref=qbuf.at[source],
            send_sem=q_send.at[target],
            recv_sem=q_recv.at[source],
            device_id=(ctx, target),
            device_id_type=MESH,
        )

    def kv_copy(d, which):
        src = (k_hbm, v_hbm)[which]
        dst = (kbuf, vbuf)[which]
        return pltpu.make_async_remote_copy(
            src_ref=src,
            dst_ref=dst.at[pl.ds(near - d * rows, rows)],
            send_sem=kv_send.at[d - 1, which],
            recv_sem=kv_recv.at[d - 1, which],
            device_id=(back(d), head),
            device_id_type=MESH,
        )

    hop1 = pltpu.make_async_remote_copy(
        src_ref=v_hbm, dst_ref=relay, send_sem=relay_send.at[0], recv_sem=relay_recv,
        device_id=(below, head), device_id_type=MESH,
    )
    hop2 = pltpu.make_async_remote_copy(
        src_ref=relay, dst_ref=vbuf.at[pl.ds(0, rows)], send_sem=relay_send.at[1], recv_sem=kv_recv.at[1, 1],
        device_id=(relay_to, head), device_id_type=MESH,
    )
    def s1_copy(j):
        return pltpu.make_async_remote_copy(
            src_ref=sink_own, dst_ref=sink_in1.at[j], send_sem=s1_send.at[j], recv_sem=s1_recv.at[j],
            device_id=(back(step1[j]), head), device_id_type=MESH,
        )

    def s2_copy(j):
        return pltpu.make_async_remote_copy(
            src_ref=sink_mid, dst_ref=sink_in2.at[j], send_sem=s2_send.at[j], recv_sem=s2_recv.at[j],
            device_id=(back(step2[j]), head), device_id_type=MESH,
        )

    for j in range(len(step1)):
        s1_copy(j).start()
    for which in (0, 1):
        kv_copy(1, which).start()
    hop1.start()
    for dz, dc in order:
        q_copy(peer(dz, dc), head).start()


    same = lambda a, b: jnp.full((2 * n, HD), a, jnp.int32) == jnp.full((2 * n, HD), b, jnp.int32)
    for j in range(len(step1)):
        s1_copy(j).wait()
    mid = sink_own[...].astype(jnp.float32)
    for j, d in enumerate(step1):
        mid = mid + jnp.where(same(last_doc[d], last_doc[0]), sink_in1[j].astype(jnp.float32), 0.0)
    sink_mid[...] = mid.astype(jnp.bfloat16)
    for j in range(len(step2)):
        s2_copy(j).start()
    hop1.wait()
    hop2.start()
    for which in (0, 1):
        kv_copy(1, which).wait()
    kv_copy(2, 0).start()
    own_q.wait()
    early = 4
    recent = rows - chunk
    pipeline(
        0, early, rows, lambda i: pl.multiple_of(near - recent + i * chunk, chunk), False, "first", True
    )
    for j in range(len(step2)):
        s2_copy(j).wait()
    got = jnp.zeros((2 * n, HD), jnp.float32)
    for j, d in enumerate(step2):
        got = got + jnp.where(same(last_doc[d], doc_a), sink_in2[j].astype(jnp.float32), 0.0)
    sink_k[pl.ds(0, n), :] = (sink_k[pl.ds(0, n), :].astype(jnp.float32) + got[:n]).astype(jnp.bfloat16)
    sink_v[pl.ds(0, n), :] = (sink_v[pl.ds(0, n), :].astype(jnp.float32) + got[n:]).astype(jnp.bfloat16)

    kv_copy(2, 0).wait()
    hop2.wait()
    pipeline(0, early, near - recent, lambda i: pl.multiple_of(i * chunk, chunk), True, "last", False)
    pipeline(early, head_n, near + chunk, lambda i: pl.multiple_of(i * chunk, chunk), True, "only", True)
    for i in range(head_n):
        o_copy(i).wait()


def per_device(ctx_n, head_n, q_rows, key_rows, value_rows, doc_lengths, window_widths, sink_widths):
    rows = key_rows.shape[0]
    chunk = q_rows.shape[0]
    docs = doc_lengths.shape[0]
    span = (WSPAN + 1) * rows
    bf = jnp.bfloat16
    n = SINK_MAX
    dma = pltpu.SemaphoreType.DMA
    return pl.pallas_call(
        functools.partial(kernel, ctx_n, head_n, docs),
        out_shape=jax.ShapeDtypeStruct((rows, QPG * HD), bf),
        in_specs=[pl.BlockSpec(memory_space=pltpu.HBM)] * 6,
        out_specs=pl.BlockSpec(memory_space=pltpu.HBM),
        scratch_shapes=[
            pltpu.VMEM((head_n, chunk, QPG * HD), bf),
            pltpu.VMEM((span, HD), bf),
            pltpu.VMEM((span, HD), bf),
            pltpu.VMEM((rows, QPG * HD), bf),
            pltpu.VMEM((2 * chunk, WSPAN * rows + chunk + HD), jnp.float32),
            pltpu.VMEM((2, WSPAN * rows + chunk + HD, chunk), bf),
            pltpu.VMEM((chunk, HD), bf),
            pltpu.VMEM((rows // HD, HD), jnp.int32),
            pltpu.VMEM((HD, HD), bf),
            pltpu.VMEM((HD, HD), bf),
            pltpu.VMEM((2 * n, HD), bf),
            pltpu.VMEM((3, 2 * n, HD), bf),
            pltpu.VMEM((2 * n, HD), bf),
            pltpu.VMEM((4, 2 * n, HD), bf),
            pltpu.VMEM((rows, HD), bf),
            pltpu.VMEM((4, chunk * QPG, 2 * HD), jnp.float32),
            pltpu.VMEM((4, chunk * QPG, HD), jnp.float32),
            pltpu.SMEM(doc_lengths.shape, jnp.int32),
            pltpu.SMEM(window_widths.shape, jnp.int32),
            pltpu.SMEM(sink_widths.shape, jnp.int32),
            dma((3,)),
            dma,
            dma((2,)),
            dma((head_n,)),
            dma((head_n,)),
            dma((2, 2)),
            dma((2, 2)),
            dma((2,)),
            dma,
            dma((3,)),
            dma((3,)),
            dma((4,)),
            dma((4,)),
            dma((head_n,)),
        ],
        compiler_params=pltpu.CompilerParams(
            collective_id=0, has_side_effects=True, vmem_limit_bytes=48 * 2**20
        ),
        cost_estimate=pl.CostEstimate(
            flops=4 * rows * QPG * HD * (WSPAN * rows + 2 * chunk),
            bytes_accessed=2 * (2 * rows * QPG * HD + 2 * rows * HD),
            transcendentals=rows * QPG * (WSPAN * rows + 2 * chunk),
        ),
        name="attention",
    )(doc_lengths, window_widths, sink_widths, q_rows, key_rows, value_rows)


def solution(mesh):
    in_specs = (P(("ctx", "head"), None), P("ctx", "head"), P("ctx", "head"), P(), P(), P())
    out_specs = P("ctx", "head")
    return jax.shard_map(
        functools.partial(per_device, mesh.shape["ctx"], mesh.shape["head"]),
        mesh=mesh, in_specs=in_specs, out_specs=out_specs, check_vma=False,
    )
```

```python
import functools

import jax
import jax.numpy as jnp
from jax import lax
from jax.experimental import pallas as pl
from jax.experimental.pallas import tpu as pltpu
from jax.sharding import PartitionSpec as P

HD = 128
QPG = 8
WSPAN = 2
SINK_MAX = 32
MESH = pl.DeviceIdType.MESH
EXP2_SCALE = HD ** (-0.5) * 1.4426950408889634
NT = (((1,), (1,)), ((), ()))
HIDDEN = -1e30


def kernel(
    ctx_n, head_n, docs,
    lengths_hbm, windows_hbm, sinks_hbm, q_hbm, k_hbm, v_hbm, out_hbm,
    qbuf, kbuf, vbuf, obuf, held, bias, ident, first_of, sink_k, sink_v, sink_own, sink_in1, sink_sum, sink_mid, sink_in2,
    relay, acc, tops, lengths, windows, sinks,
    small_local, q_local, kv_local, q_send, q_recv, kv_send, kv_recv, relay_send, relay_recv,
    s1_send, s1_recv, s2_send, s2_recv, o_sem,
):
    ctx = lax.axis_index("ctx")
    head = lax.axis_index("head")
    rows = k_hbm.shape[0]
    chunk = q_hbm.shape[0]
    width = QPG * HD
    near = WSPAN * rows
    z, core, zn = head // 2, head % 2, head_n // 2
    base = ctx * rows

    def back_of(c):
        return lax.rem(c + ctx_n, ctx_n)

    def back(d):
        return back_of(ctx + d)

    step1 = (1, 2, 3, 4)
    stride = 4
    step2 = (4, 8, 12)
    order = [(dz, dc) for dz, dc in ((0, 1), (1, 0), (3, 0), (1, 1), (3, 1), (2, 0), (2, 1))]

    x, y = ctx // stride, ctx % stride
    below = x * stride + lax.rem(y + stride - 1, stride)
    above = x * stride + lax.rem(y + 1, stride)
    two_back = back_of(ctx - 2)
    relay_from = two_back // stride * stride + lax.rem(two_back + stride - 1, stride)
    last = ctx_n - 1

    def peer(dz, dc):
        return lax.rem(z + dz, zn) * 2 + lax.rem(core + dc, 2)

    barrier = pltpu.get_barrier_semaphore()
    def greet(c):
        pl.semaphore_signal(barrier, inc=1, device_id=(c, head), device_id_type=MESH)

    for d in step1 + step2[1:]:
        pl.when(ctx >= d)(functools.partial(greet, back(-d)))
    pl.when(ctx >= 2)(functools.partial(greet, relay_from))
    pl.when(above + 2 <= last)(functools.partial(greet, above))
    to_ctx = jnp.minimum(last - ctx, len(step1)) + sum(jnp.where(ctx + d <= last, 1, 0) for d in step2[1:])
    to_ctx = to_ctx + jnp.where(ctx + 2 <= last, 1, 0) + jnp.where(above + 2 <= last, 1, 0)
    for dz, dc in order:
        pl.semaphore_signal(barrier, inc=1, device_id=(ctx, peer(dz, dc)), device_id_type=MESH)

    own_q = pltpu.make_async_copy(
        q_hbm.at[:, pl.ds(pl.multiple_of(head * width, width), width)], qbuf.at[head], q_local
    )
    own_k = pltpu.make_async_copy(k_hbm, kbuf.at[pl.ds(near, rows)], kv_local.at[0])
    own_v = pltpu.make_async_copy(v_hbm, vbuf.at[pl.ds(near, rows)], kv_local.at[1])
    small = [
        pltpu.make_async_copy(src, dst, small_local.at[j])
        for j, (src, dst) in enumerate(((lengths_hbm, lengths), (windows_hbm, windows), (sinks_hbm, sinks)))
    ]
    for copy in small:
        copy.start()
    own_k.start()
    own_v.start()
    own_q.start()
    for copy in small:
        copy.wait()

    starts = []
    running = jnp.int32(0)
    for d in range(docs):
        starts.append(running)
        running = running + lengths[d]

    def start_of(position):
        found = jnp.int32(-1)
        for s in starts:
            found = jnp.where(position >= s, s, found)
        return found

    window = windows[head]
    sink_width = sinks[head]
    last_doc = {d: start_of(base - d * rows + rows - 1) for d in (0,) + step1}
    doc_before = {d: start_of(base - d * rows) for d in step2}
    doc_a = start_of(base)
    doc_b = start_of(base + rows // 2 - 1)
    doc_b = jnp.where(doc_b > base, doc_b, -1)

    iota_r = lax.broadcasted_iota(jnp.int32, (chunk, HD), 0)
    iota_c = lax.broadcasted_iota(jnp.int32, (chunk, HD), 1)
    ident[...] = jnp.where(iota_r == iota_c, 1.0, 0.0).astype(jnp.bfloat16)
    grid_pos = base + lax.broadcasted_iota(jnp.int32, (rows // HD, HD), 0) * HD + lax.broadcasted_iota(
        jnp.int32, (rows // HD, HD), 1
    )
    found = jnp.zeros((rows // HD, HD), jnp.int32)
    for s in starts:
        found = jnp.where(grid_pos >= s, s, found)
    first_of[...] = found
    @pl.when(ctx == 0)
    def _():
        kbuf[pl.ds(rows, rows), :] = jnp.zeros((rows, HD), jnp.bfloat16)
        vbuf[pl.ds(rows, rows), :] = jnp.zeros((rows, HD), jnp.bfloat16)

    @pl.when(ctx < 2)
    def _():
        kbuf[pl.ds(0, rows), :] = jnp.zeros((rows, HD), jnp.bfloat16)
        vbuf[pl.ds(0, rows), :] = jnp.zeros((rows, HD), jnp.bfloat16)

    sink_k[...] = jnp.zeros_like(sink_k)
    sink_v[...] = jnp.zeros_like(sink_v)

    n = SINK_MAX
    srank = lax.broadcasted_iota(jnp.int32, (HD, chunk), 0)

    def place(s):
        dz = jnp.where(s < 2, 0, jnp.where(s < 6, 1 + 2 * (s % 2), 2))
        dc = jnp.where(s < 2, s, jnp.where(s < 6, s // 2 - 1, s - 6))
        return peer(dz, dc)

    def limits(i):
        t = base + i * chunk + lax.broadcasted_iota(jnp.int32, (1, chunk), 1)
        first = first_of[pl.ds(i, 1), :]
        return t, first, jnp.maximum(first, t - window + 1)

    def set_sink_bias(slot, at, t, first):
        doc = jnp.where(srank < n, doc_a, jnp.where(srank < 2 * n, doc_b, -1))
        r = srank % n
        seen = (r < sink_width) & (doc == first) & (doc + r <= t - window)
        bias[slot, pl.ds(at, HD), :] = jnp.where(seen, 0.0, HIDDEN).astype(jnp.bfloat16)

    def pipeline(lo, hi, reach, row_of, with_sinks, stage, wait_queries, on_the_way=()):
        total = reach + (HD if with_sinks else 0)

        def set_bias(i, slot):
            t, first, low = limits(i)
            kp = base - near + row_of(i) + lax.broadcasted_iota(jnp.int32, (reach, chunk), 0)
            bias[slot, pl.ds(0, reach), :] = jnp.where((kp <= t) & (kp >= low), 0.0, HIDDEN).astype(jnp.bfloat16)
            if with_sinks:
                set_sink_bias(slot, reach, t, first)

        def score(i, slot, h):
            keys = kbuf[pl.ds(row_of(i), reach), :]
            if with_sinks:
                keys = jnp.concatenate([keys, sink_k[...]], axis=0)
            keys = jnp.concatenate([keys, bias[slot, pl.ds(0, total), :]], axis=1)
            unit = ident[...]
            left = jnp.concatenate(
                [jnp.concatenate([qbuf[i, :, a * HD : (a + 1) * HD], unit], axis=1) for a in (h, h + 1)], axis=0
            )
            return lax.dot_general(left, keys, NT, preferred_element_type=jnp.float32)

        def finish(s, i, h, scores):
            vals = vbuf[pl.ds(row_of(i), reach), :]
            if with_sinks:
                vals = jnp.concatenate([vals, sink_v[...]], axis=0)
            vals = jnp.concatenate([vals, jnp.ones((total, HD), jnp.bfloat16)], axis=1)
            span = pl.ds(h * chunk, 2 * chunk)
            top = jnp.max(scores, axis=1, keepdims=True)
            if stage == "last":
                old = tops[s, span, :]
                top = jnp.maximum(old[:, :1], top)
            raw = jnp.exp2(scores * EXP2_SCALE - top * EXP2_SCALE).astype(jnp.bfloat16)
            summed = jnp.dot(raw, vals, preferred_element_type=jnp.float32)
            if stage == "first":
                tops[s, span, :] = jnp.broadcast_to(top, (2 * chunk, HD))
                acc[s, span, :] = summed
                return
            if stage == "last":
                factor = jnp.exp2(old * EXP2_SCALE - jnp.broadcast_to(top * EXP2_SCALE, (2 * chunk, HD)))
                summed = summed + acc[s, span, :] * jnp.concatenate([factor, factor], axis=1)
            result = (summed[:, :HD] / summed[:, HD:]).astype(jnp.bfloat16)
            for a in (0, 1):
                obuf[pl.ds(pl.multiple_of(i * chunk, chunk), chunk), (h + a) * HD : (h + a + 1) * HD] = result[
                    a * chunk : (a + 1) * chunk
                ]

        def body(s, carry):
            slot = lax.rem(s - lo, 2)
            later = jnp.where(s + 1 < hi, s + 1, s)
            i, j = place(s), place(later)
            for k, action in enumerate(on_the_way):
                pl.when(s == lo + k)(action)
            if wait_queries:

                @pl.when(s + 1 < hi)
                def _():
                    q_copy(j, j).wait_recv()

            set_bias(j, 1 - slot)
            scores = held[:, pl.ds(0, total)]
            for h in range(0, QPG, 2):
                ahead = score(i, slot, h + 2) if h + 2 < QPG else score(j, 1 - slot, 0)
                finish(s, i, h, scores)
                scores = ahead
            held[:, pl.ds(0, total)] = scores
            if stage != "first":
                o_copy(i).start()
            return carry

        i = place(lo)
        if wait_queries and lo > 0:
            q_copy(i, i).wait_recv()
        set_bias(i, 0)
        held[:, pl.ds(0, total)] = score(i, 0, 0)
        lax.fori_loop(lo, hi, body, 0)

    def o_copy(i):
        span = pl.ds(pl.multiple_of(i * chunk, chunk), chunk)
        return pltpu.make_async_copy(obuf.at[span], out_hbm.at[span], o_sem.at[i])

    own_k.wait()
    own_v.wait()
    at = base + lax.broadcasted_iota(jnp.int32, (SINK_MAX, rows), 1)
    rank = lax.broadcasted_iota(jnp.int32, (SINK_MAX, rows), 0)
    pick = jnp.concatenate(
        [jnp.where(at == s + rank, 1.0, 0.0).astype(jnp.bfloat16) for s in (last_doc[0], doc_a, doc_b)], axis=0
    )
    own = jnp.concatenate([kbuf[pl.ds(near, rows), :], vbuf[pl.ds(near, rows), :]], axis=1)
    picked = jnp.dot(pick, own, preferred_element_type=jnp.float32).astype(jnp.bfloat16)
    sink_own[pl.ds(0, n), :] = picked[:n, :HD]
    sink_own[pl.ds(n, n), :] = picked[:n, HD:]
    sink_k[pl.ds(0, n), :] = picked[n : 2 * n, :HD]
    sink_v[pl.ds(0, n), :] = picked[n : 2 * n, HD:]
    sink_k[pl.ds(n, n), :] = picked[2 * n : 3 * n, :HD]
    sink_v[pl.ds(n, n), :] = picked[2 * n : 3 * n, HD:]

    pl.semaphore_wait(barrier, len(order) + to_ctx)

    def q_copy(target, source):
        return pltpu.make_async_remote_copy(
            src_ref=q_hbm.at[:, pl.ds(pl.multiple_of(target * width, width), width)],
            dst_ref=qbuf.at[source],
            send_sem=q_send.at[target],
            recv_sem=q_recv.at[source],
            device_id=(ctx, target),
            device_id_type=MESH,
        )

    cut = 3 * chunk

    def kv_copy(d, which, lo, count, sem):
        src = (k_hbm, v_hbm)[which]
        dst = (kbuf, vbuf)[which]
        return pltpu.make_async_remote_copy(
            src_ref=src.at[pl.ds(lo, count)],
            dst_ref=dst.at[pl.ds(near - d * rows + lo, count)],
            send_sem=kv_send.at[sem, which],
            recv_sem=kv_recv.at[sem, which],
            device_id=(back(d), head),
            device_id_type=MESH,
        )

    def late_rows(which):
        return kv_copy(1, which, cut, rows - cut, 0)

    def early_rows(which):
        return kv_copy(1, which, 0, cut, 2)

    far_keys = kv_copy(2, 0, 0, rows, 1)

    hop1 = pltpu.make_async_remote_copy(
        src_ref=v_hbm, dst_ref=relay, send_sem=relay_send.at[0], recv_sem=relay_recv,
        device_id=(below, head), device_id_type=MESH,
    )
    hop2 = pltpu.make_async_remote_copy(
        src_ref=relay, dst_ref=vbuf.at[pl.ds(0, rows)], send_sem=relay_send.at[1], recv_sem=kv_recv.at[1, 1],
        device_id=(back_of(above + 2), head), device_id_type=MESH,
    )
    def s1_copy(d):
        return pltpu.make_async_remote_copy(
            src_ref=sink_own, dst_ref=sink_in1.at[d - 1], send_sem=s1_send.at[d - 1], recv_sem=s1_recv.at[d - 1],
            device_id=(back(d), head), device_id_type=MESH,
        )

    def s2_copy(j):
        return pltpu.make_async_remote_copy(
            src_ref=sink_mid, dst_ref=sink_in2.at[j], send_sem=s2_send.at[j], recv_sem=s2_recv.at[j],
            device_id=(back(step2[j]), head), device_id_type=MESH,
        )

    @pl.when(ctx < last)
    def _():
        for d in step1:
            pl.when(ctx + d <= last)(s1_copy(d).start)
        for which in (0, 1):
            late_rows(which).start()
        for which in (0, 1):
            early_rows(which).start()

    pl.when(ctx + 2 <= last)(hop1.start)
    for dz, dc in order[:5]:
        q_copy(peer(dz, dc), head).start()

    same = lambda a, b: jnp.full((2 * n, HD), a, jnp.int32) == jnp.full((2 * n, HD), b, jnp.int32)
    sink_sum[pl.ds(0, n), :] = sink_k[pl.ds(0, n), :].astype(jnp.float32)
    sink_sum[pl.ds(n, n), :] = sink_v[pl.ds(0, n), :].astype(jnp.float32)
    for d in step1:

        @pl.when(ctx >= d)
        def _(d=d):
            s1_copy(d).wait_recv()
            take = same(last_doc[d], doc_a)
            if d == stride:
                take = take & (same(doc_before[d], doc_a) == False)
            sink_sum[...] += jnp.where(take, sink_in1[d - 1].astype(jnp.float32), 0.0)

    def relay_on():
        hop1.wait_recv()
        hop2.start()

    pl.when(above + 2 <= last)(relay_on)

    sink_mid[...] = sink_sum[...].astype(jnp.bfloat16)
    for j, d in enumerate(step2):
        pl.when(ctx + d <= last)(s2_copy(j).start)

    def send_far_keys():
        @pl.when(ctx < last)
        def _():
            for which in (0, 1):
                late_rows(which).wait_send()
                early_rows(which).wait_send()

        pl.when(ctx + 2 <= last)(far_keys.start)

    def send_far_queries():
        for dz, dc in order[1:5]:
            q_copy(peer(dz, dc), head).wait_send()
        for dz, dc in order[5:]:
            q_copy(peer(dz, dc), head).start()

    def at_block(i, blocks):
        return pl.multiple_of(i * chunk + blocks * chunk, chunk)

    @pl.when(ctx >= 1)
    def _():
        for which in (0, 1):
            late_rows(which).wait_recv()

    own_q.wait()
    per_shard = rows // chunk
    first_reach = per_shard - cut // chunk
    early, middle = 4, 6
    pipeline(
        0, early, (first_reach + 1) * chunk, lambda i: at_block(i, 2 * per_shard - first_reach), False, "first", True,
        (lambda: None, send_far_keys, send_far_queries),
    )

    @pl.when(ctx >= 1)
    def _():
        for which in (0, 1):
            early_rows(which).wait_recv()

    for j, d in enumerate(step2):

        @pl.when(ctx >= d)
        def _(j=j, d=d):
            s2_copy(j).wait_recv()
            sink_sum[...] += jnp.where(same(doc_before[d], doc_a), sink_in2[j].astype(jnp.float32), 0.0)

    sink_k[pl.ds(0, n), :] = sink_sum[pl.ds(0, n), :].astype(jnp.bfloat16)
    sink_v[pl.ds(0, n), :] = sink_sum[pl.ds(n, n), :].astype(jnp.bfloat16)

    pipeline(early, middle, rows + chunk, lambda i: at_block(i, per_shard), True, "first", True)

    @pl.when(ctx >= 2)
    def _():
        far_keys.wait_recv()
        hop2.wait_recv()

    pipeline(0, early, near - first_reach * chunk, lambda i: at_block(i, 0), True, "last", False)
    pipeline(early, middle, rows, lambda i: at_block(i, 0), False, "last", False)
    pipeline(middle, head_n, near + chunk, lambda i: at_block(i, 0), True, "only", True)
    for i in range(head_n):
        o_copy(i).wait()

    for d in step1:
        pl.when(ctx + d <= last)(s1_copy(d).wait_send)
    for j, d in enumerate(step2):
        pl.when(ctx + d <= last)(s2_copy(j).wait_send)

    for dz, dc in order[:1] + order[5:]:
        q_copy(peer(dz, dc), head).wait_send()

    @pl.when(ctx + 2 <= last)
    def _():
        far_keys.wait_send()
        hop1.wait_send()

    pl.when(above + 2 <= last)(hop2.wait_send)


def per_device(ctx_n, head_n, q_rows, key_rows, value_rows, doc_lengths, window_widths, sink_widths):
    rows = key_rows.shape[0]
    chunk = q_rows.shape[0]
    docs = doc_lengths.shape[0]
    span = (WSPAN + 1) * rows
    bf = jnp.bfloat16
    n = SINK_MAX
    dma = pltpu.SemaphoreType.DMA
    return pl.pallas_call(
        functools.partial(kernel, ctx_n, head_n, docs),
        out_shape=pltpu.VMEM((rows, QPG * HD), bf),
        in_specs=[pl.BlockSpec(memory_space=pltpu.HBM)] * 6,
        out_specs=pl.BlockSpec(memory_space=pl.ANY),
        scratch_shapes=[
            pltpu.VMEM((head_n, chunk, QPG * HD), bf),
            pltpu.VMEM((span, HD), bf),
            pltpu.VMEM((span, HD), bf),
            pltpu.VMEM((rows, QPG * HD), bf),
            pltpu.VMEM((2 * chunk, WSPAN * rows + chunk + HD), jnp.float32),
            pltpu.VMEM((2, WSPAN * rows + chunk + HD, chunk), bf),
            pltpu.VMEM((chunk, HD), bf),
            pltpu.VMEM((rows // HD, HD), jnp.int32),
            pltpu.VMEM((HD, HD), bf),
            pltpu.VMEM((HD, HD), bf),
            pltpu.VMEM((2 * n, HD), bf),
            pltpu.VMEM((4, 2 * n, HD), bf),
            pltpu.VMEM((2 * n, HD), jnp.float32),
            pltpu.VMEM((2 * n, HD), bf),
            pltpu.VMEM((3, 2 * n, HD), bf),
            pltpu.VMEM((rows, HD), bf),
            pltpu.VMEM((6, chunk * QPG, 2 * HD), jnp.float32),
            pltpu.VMEM((6, chunk * QPG, HD), jnp.float32),
            pltpu.SMEM(doc_lengths.shape, jnp.int32),
            pltpu.SMEM(window_widths.shape, jnp.int32),
            pltpu.SMEM(sink_widths.shape, jnp.int32),
            dma((3,)),
            dma,
            dma((2,)),
            dma((head_n,)),
            dma((head_n,)),
            dma((3, 2)),
            dma((3, 2)),
            dma((2,)),
            dma,
            dma((4,)),
            dma((4,)),
            dma((3,)),
            dma((3,)),
            dma((head_n,)),
        ],
        compiler_params=pltpu.CompilerParams(
            collective_id=0, has_side_effects=True, vmem_limit_bytes=56 * 2**20
        ),
        cost_estimate=pl.CostEstimate(
            flops=4 * rows * QPG * HD * (WSPAN * rows + 2 * chunk),
            bytes_accessed=2 * (2 * rows * QPG * HD + 2 * rows * HD),
            transcendentals=rows * QPG * (WSPAN * rows + 2 * chunk),
        ),
        name="attention",
    )(*[
        pltpu.with_memory_space_constraint(a, pltpu.HBM)
        for a in (doc_lengths, window_widths, sink_widths, q_rows, key_rows, value_rows)
    ])


def solution(mesh):
    in_specs = (P(("ctx", "head"), None), P("ctx", "head"), P("ctx", "head"), P(), P(), P())
    out_specs = P("ctx", "head")
    return jax.shard_map(
        functools.partial(per_device, mesh.shape["ctx"], mesh.shape["head"]),
        mesh=mesh, in_specs=in_specs, out_specs=out_specs, check_vma=False,
    )
```

```python
import functools

import jax
import jax.numpy as jnp
from jax import lax
from jax.experimental import pallas as pl
from jax.experimental.pallas import tpu as pltpu
from jax.sharding import PartitionSpec as P

HD = 128
QPG = 8
WSPAN = 2
SINK_MAX = 32
MESH = pl.DeviceIdType.MESH
EXP2_SCALE = HD ** (-0.5) * 1.4426950408889634
NT = (((1,), (1,)), ((), ()))
HIDDEN = -1e30


def kernel(
    ctx_n, head_n, docs,
    lengths_hbm, windows_hbm, sinks_hbm, q_hbm, k_hbm, v_hbm, out_hbm,
    qbuf, kbuf, vbuf, obuf, held, bias, ident, first_of, sink_k, sink_v, sink_own, sink_in1, sink_sum, sink_mid, sink_in2,
    relay, acc, tops, lengths, windows, sinks,
    small_local, q_local, kv_local, q_send, q_recv, kv_send, kv_recv, relay_send, relay_recv,
    s1_send, s1_recv, s2_send, s2_recv, o_sem,
):
    ctx = lax.axis_index("ctx")
    head = lax.axis_index("head")
    rows = k_hbm.shape[0]
    chunk = q_hbm.shape[0]
    width = QPG * HD
    near = WSPAN * rows
    z, core, zn = head // 2, head % 2, head_n // 2
    base = ctx * rows

    def back_of(c):
        return lax.rem(c + ctx_n, ctx_n)

    def back(d):
        return back_of(ctx + d)

    step1 = (1, 2, 3, 4)
    stride = 4
    step2 = (4, 8, 12)
    order = [(dz, dc) for dz, dc in ((0, 1), (1, 0), (3, 0), (1, 1), (3, 1), (2, 0), (2, 1))]

    x, y = ctx // stride, ctx % stride
    below = x * stride + lax.rem(y + stride - 1, stride)
    above = x * stride + lax.rem(y + 1, stride)
    two_back = back_of(ctx - 2)
    relay_from = two_back // stride * stride + lax.rem(two_back + stride - 1, stride)
    last = ctx_n - 1

    def peer(dz, dc):
        return lax.rem(z + dz, zn) * 2 + lax.rem(core + dc, 2)

    barrier = pltpu.get_barrier_semaphore()
    def greet(c):
        pl.semaphore_signal(barrier, inc=1, device_id=(c, head), device_id_type=MESH)

    for d in step1 + step2[1:]:
        pl.when(ctx >= d)(functools.partial(greet, back(-d)))
    pl.when(ctx >= 2)(functools.partial(greet, relay_from))
    pl.when(above + 2 <= last)(functools.partial(greet, above))
    to_ctx = jnp.minimum(last - ctx, len(step1)) + sum(jnp.where(ctx + d <= last, 1, 0) for d in step2[1:])
    to_ctx = to_ctx + jnp.where(ctx + 2 <= last, 1, 0) + jnp.where(above + 2 <= last, 1, 0)
    for dz, dc in order:
        pl.semaphore_signal(barrier, inc=1, device_id=(ctx, peer(dz, dc)), device_id_type=MESH)

    own_q = pltpu.make_async_copy(
        q_hbm.at[:, pl.ds(pl.multiple_of(head * width, width), width)], qbuf.at[head], q_local
    )
    own_k = pltpu.make_async_copy(k_hbm, kbuf.at[pl.ds(near, rows)], kv_local.at[0])
    own_v = pltpu.make_async_copy(v_hbm, vbuf.at[pl.ds(near, rows)], kv_local.at[1])
    small = [
        pltpu.make_async_copy(src, dst, small_local.at[j])
        for j, (src, dst) in enumerate(((lengths_hbm, lengths), (windows_hbm, windows), (sinks_hbm, sinks)))
    ]
    for copy in small:
        copy.start()
    own_k.start()
    own_v.start()
    own_q.start()
    for copy in small:
        copy.wait()

    starts = []
    running = jnp.int32(0)
    for d in range(docs):
        starts.append(running)
        running = running + lengths[d]

    def start_of(position):
        found = jnp.int32(-1)
        for s in starts:
            found = jnp.where(position >= s, s, found)
        return found

    window = windows[head]
    sink_width = sinks[head]
    last_doc = {d: start_of(base - d * rows + rows - 1) for d in (0,) + step1}
    doc_before = {d: start_of(base - d * rows) for d in step2}
    doc_a = start_of(base)
    doc_b = start_of(base + rows // 2 - 1)
    doc_b = jnp.where(doc_b > base, doc_b, -1)

    iota_r = lax.broadcasted_iota(jnp.int32, (chunk, HD), 0)
    iota_c = lax.broadcasted_iota(jnp.int32, (chunk, HD), 1)
    ident[...] = jnp.where(iota_r == iota_c, 1.0, 0.0).astype(jnp.bfloat16)
    grid_pos = base + lax.broadcasted_iota(jnp.int32, (rows // HD, HD), 0) * HD + lax.broadcasted_iota(
        jnp.int32, (rows // HD, HD), 1
    )
    found = jnp.zeros((rows // HD, HD), jnp.int32)
    for s in starts:
        found = jnp.where(grid_pos >= s, s, found)
    first_of[...] = found
    @pl.when(ctx == 0)
    def _():
        kbuf[pl.ds(rows, rows), :] = jnp.zeros((rows, HD), jnp.bfloat16)
        vbuf[pl.ds(rows, rows), :] = jnp.zeros((rows, HD), jnp.bfloat16)

    @pl.when(ctx < 2)
    def _():
        kbuf[pl.ds(0, rows), :] = jnp.zeros((rows, HD), jnp.bfloat16)
        vbuf[pl.ds(0, rows), :] = jnp.zeros((rows, HD), jnp.bfloat16)

    sink_k[...] = jnp.zeros_like(sink_k)
    sink_v[...] = jnp.zeros_like(sink_v)

    n = SINK_MAX
    srank = lax.broadcasted_iota(jnp.int32, (HD, chunk), 0)

    def place(s):
        dz = jnp.where(s < 2, 0, jnp.where(s < 6, 1 + 2 * (s % 2), 2))
        dc = jnp.where(s < 2, s, jnp.where(s < 6, s // 2 - 1, s - 6))
        return peer(dz, dc)

    def limits(i):
        t = base + i * chunk + lax.broadcasted_iota(jnp.int32, (1, chunk), 1)
        first = first_of[pl.ds(i, 1), :]
        return t, first, jnp.maximum(first, t - window + 1)

    def set_sink_bias(slot, at, t, first):
        doc = jnp.where(srank < n, doc_a, jnp.where(srank < 2 * n, doc_b, -1))
        r = srank % n
        seen = (r < sink_width) & (doc == first) & (doc + r <= t - window)
        bias[slot, pl.ds(at, HD), :] = jnp.where(seen, 0.0, HIDDEN).astype(jnp.bfloat16)

    def pipeline(lo, hi, reach, row_of, with_sinks, stage, wait_queries, on_the_way=()):
        total = reach + (HD if with_sinks else 0)

        def set_bias(i, slot):
            t, first, low = limits(i)
            kp = base - near + row_of(i) + lax.broadcasted_iota(jnp.int32, (reach, chunk), 0)
            bias[slot, pl.ds(0, reach), :] = jnp.where((kp <= t) & (kp >= low), 0.0, HIDDEN).astype(jnp.bfloat16)
            if with_sinks:
                set_sink_bias(slot, reach, t, first)

        def score(i, slot, h):
            keys = kbuf[pl.ds(row_of(i), reach), :]
            if with_sinks:
                keys = jnp.concatenate([keys, sink_k[...]], axis=0)
            keys = jnp.concatenate([keys, bias[slot, pl.ds(0, total), :]], axis=1)
            unit = ident[...]
            left = jnp.concatenate(
                [jnp.concatenate([qbuf[i, :, a * HD : (a + 1) * HD], unit], axis=1) for a in (h, h + 1)], axis=0
            )
            return lax.dot_general(left, keys, NT, preferred_element_type=jnp.float32)

        def finish(s, i, h, scores):
            vals = vbuf[pl.ds(row_of(i), reach), :]
            if with_sinks:
                vals = jnp.concatenate([vals, sink_v[...]], axis=0)
            vals = jnp.concatenate([vals, jnp.ones((total, HD), jnp.bfloat16)], axis=1)
            span = pl.ds(h * chunk, 2 * chunk)
            top = jnp.max(scores, axis=1, keepdims=True)
            if stage == "last":
                old = tops[s, span, :]
                top = jnp.maximum(old[:, :1], top)
            raw = jnp.exp2(scores * EXP2_SCALE - top * EXP2_SCALE).astype(jnp.bfloat16)
            summed = jnp.dot(raw, vals, preferred_element_type=jnp.float32)
            if stage == "first":
                tops[s, span, :] = jnp.broadcast_to(top, (2 * chunk, HD))
                acc[s, span, :] = summed
                return
            if stage == "last":
                factor = jnp.exp2(old * EXP2_SCALE - jnp.broadcast_to(top * EXP2_SCALE, (2 * chunk, HD)))
                summed = summed + acc[s, span, :] * jnp.concatenate([factor, factor], axis=1)
            result = (summed[:, :HD] / summed[:, HD:]).astype(jnp.bfloat16)
            for a in (0, 1):
                obuf[pl.ds(pl.multiple_of(i * chunk, chunk), chunk), (h + a) * HD : (h + a + 1) * HD] = result[
                    a * chunk : (a + 1) * chunk
                ]

        def wait_for(s):
            if wait_queries:
                i = place(s)
                q_copy(i, i).wait_recv()

        def body(step, carry):
            s = lo + 2 * step
            more = s + 2 < hi
            later = jnp.where(more, s + 2, s + 1)
            for k, action in enumerate(on_the_way):
                pl.when(step == k)(action)
            wait_for(s + 1)
            if hi - lo > 2:
                pl.when(more)(functools.partial(wait_for, s + 2))
            set_bias(place(s + 1), 1)
            tiles = [(s + d, place(s + d), d, h) for d in (0, 1) for h in range(0, QPG, 2)]
            scores = held[:, pl.ds(0, total)]
            for at, (chunk_s, i, slot, h) in enumerate(tiles):
                if at + 1 < len(tiles):
                    ahead = score(tiles[at + 1][1], tiles[at + 1][2], tiles[at + 1][3])
                elif hi - lo > 2:
                    set_bias(place(later), 0)
                    ahead = score(place(later), 0, 0)
                finish(chunk_s, i, h, scores)
                scores = ahead
                if stage != "first" and h + 2 == QPG:
                    o_copy(i).start()
            if hi - lo > 2:
                held[:, pl.ds(0, total)] = scores
            return carry

        if lo > 0:
            wait_for(lo)
        set_bias(place(lo), 0)
        held[:, pl.ds(0, total)] = score(place(lo), 0, 0)
        if hi - lo > 2:
            lax.fori_loop(0, (hi - lo) // 2, body, 0)
        else:
            body(0, 0)

    def o_copy(i):
        span = pl.ds(pl.multiple_of(i * chunk, chunk), chunk)
        return pltpu.make_async_copy(obuf.at[span], out_hbm.at[span], o_sem.at[i])

    own_k.wait()
    own_v.wait()
    at = base + lax.broadcasted_iota(jnp.int32, (SINK_MAX, rows), 1)
    rank = lax.broadcasted_iota(jnp.int32, (SINK_MAX, rows), 0)
    pick = jnp.concatenate(
        [jnp.where(at == s + rank, 1.0, 0.0).astype(jnp.bfloat16) for s in (last_doc[0], doc_a, doc_b)], axis=0
    )
    own = jnp.concatenate([kbuf[pl.ds(near, rows), :], vbuf[pl.ds(near, rows), :]], axis=1)
    picked = jnp.dot(pick, own, preferred_element_type=jnp.float32).astype(jnp.bfloat16)
    sink_own[pl.ds(0, n), :] = picked[:n, :HD]
    sink_own[pl.ds(n, n), :] = picked[:n, HD:]
    sink_k[pl.ds(0, n), :] = picked[n : 2 * n, :HD]
    sink_v[pl.ds(0, n), :] = picked[n : 2 * n, HD:]
    sink_k[pl.ds(n, n), :] = picked[2 * n : 3 * n, :HD]
    sink_v[pl.ds(n, n), :] = picked[2 * n : 3 * n, HD:]

    pl.semaphore_wait(barrier, len(order) + to_ctx)

    def q_copy(target, source):
        return pltpu.make_async_remote_copy(
            src_ref=q_hbm.at[:, pl.ds(pl.multiple_of(target * width, width), width)],
            dst_ref=qbuf.at[source],
            send_sem=q_send.at[target],
            recv_sem=q_recv.at[source],
            device_id=(ctx, target),
            device_id_type=MESH,
        )

    cut = 3 * chunk

    def kv_copy(d, which, lo, count, sem):
        src = (k_hbm, v_hbm)[which]
        dst = (kbuf, vbuf)[which]
        return pltpu.make_async_remote_copy(
            src_ref=src.at[pl.ds(lo, count)],
            dst_ref=dst.at[pl.ds(near - d * rows + lo, count)],
            send_sem=kv_send.at[sem, which],
            recv_sem=kv_recv.at[sem, which],
            device_id=(back(d), head),
            device_id_type=MESH,
        )

    def late_rows(which):
        return kv_copy(1, which, cut, rows - cut, 0)

    def early_rows(which):
        return kv_copy(1, which, 0, cut, 2)

    far_keys = kv_copy(2, 0, 0, rows, 1)

    hop1 = pltpu.make_async_remote_copy(
        src_ref=v_hbm, dst_ref=relay, send_sem=relay_send.at[0], recv_sem=relay_recv,
        device_id=(below, head), device_id_type=MESH,
    )
    hop2 = pltpu.make_async_remote_copy(
        src_ref=relay, dst_ref=vbuf.at[pl.ds(0, rows)], send_sem=relay_send.at[1], recv_sem=kv_recv.at[1, 1],
        device_id=(back_of(above + 2), head), device_id_type=MESH,
    )
    def s1_copy(d):
        return pltpu.make_async_remote_copy(
            src_ref=sink_own, dst_ref=sink_in1.at[d - 1], send_sem=s1_send.at[d - 1], recv_sem=s1_recv.at[d - 1],
            device_id=(back(d), head), device_id_type=MESH,
        )

    def s2_copy(j):
        return pltpu.make_async_remote_copy(
            src_ref=sink_mid, dst_ref=sink_in2.at[j], send_sem=s2_send.at[j], recv_sem=s2_recv.at[j],
            device_id=(back(step2[j]), head), device_id_type=MESH,
        )

    @pl.when(ctx < last)
    def _():
        for d in step1:
            pl.when(ctx + d <= last)(s1_copy(d).start)
        for which in (0, 1):
            late_rows(which).start()
        for which in (0, 1):
            early_rows(which).start()

    pl.when(ctx + 2 <= last)(hop1.start)
    for dz, dc in order[:5]:
        q_copy(peer(dz, dc), head).start()

    same = lambda a, b: jnp.full((2 * n, HD), a, jnp.int32) == jnp.full((2 * n, HD), b, jnp.int32)
    sink_sum[pl.ds(0, n), :] = sink_k[pl.ds(0, n), :].astype(jnp.float32)
    sink_sum[pl.ds(n, n), :] = sink_v[pl.ds(0, n), :].astype(jnp.float32)
    for d in step1:

        @pl.when(ctx >= d)
        def _(d=d):
            s1_copy(d).wait_recv()
            take = same(last_doc[d], doc_a)
            if d == stride:
                take = take & (same(doc_before[d], doc_a) == False)
            sink_sum[...] += jnp.where(take, sink_in1[d - 1].astype(jnp.float32), 0.0)

    sink_mid[...] = sink_sum[...].astype(jnp.bfloat16)
    for j, d in enumerate(step2):
        pl.when(ctx + d <= last)(s2_copy(j).start)

    def send_far_keys():
        @pl.when(ctx < last)
        def _():
            for which in (0, 1):
                late_rows(which).wait_send()
                early_rows(which).wait_send()

        pl.when(ctx + 2 <= last)(far_keys.start)

    def send_far_queries():
        for dz, dc in order[1:5]:
            q_copy(peer(dz, dc), head).wait_send()
        for dz, dc in order[5:]:
            q_copy(peer(dz, dc), head).start()

    def at_block(i, blocks):
        return pl.multiple_of(i * chunk + blocks * chunk, chunk)

    def relay_on():
        hop1.wait_recv()
        hop2.start()

    pl.when(above + 2 <= last)(relay_on)

    @pl.when(ctx >= 1)
    def _():
        for which in (0, 1):
            late_rows(which).wait_recv()

    own_q.wait()
    per_shard = rows // chunk
    first_reach = per_shard - cut // chunk
    early, middle = 2, 6
    pipeline(
        0, early, (first_reach + 1) * chunk, lambda i: at_block(i, 2 * per_shard - first_reach), False, "first", True
    )

    @pl.when(ctx >= 1)
    def _():
        for which in (0, 1):
            early_rows(which).wait_recv()

    for j, d in enumerate(step2):

        @pl.when(ctx >= d)
        def _(j=j, d=d):
            s2_copy(j).wait_recv()
            sink_sum[...] += jnp.where(same(doc_before[d], doc_a), sink_in2[j].astype(jnp.float32), 0.0)

    sink_k[pl.ds(0, n), :] = sink_sum[pl.ds(0, n), :].astype(jnp.bfloat16)
    sink_v[pl.ds(0, n), :] = sink_sum[pl.ds(n, n), :].astype(jnp.bfloat16)

    send_far_keys()
    pipeline(
        early, middle, rows + chunk, lambda i: at_block(i, per_shard), True, "first", True,
        (lambda: None, send_far_queries),
    )

    @pl.when(ctx >= 2)
    def _():
        far_keys.wait_recv()
        hop2.wait_recv()

    pipeline(0, early, near - first_reach * chunk, lambda i: at_block(i, 0), True, "last", False)
    pipeline(early, middle, rows, lambda i: at_block(i, 0), False, "last", False)
    pipeline(middle, head_n, near + chunk, lambda i: at_block(i, 0), True, "only", True)
    for i in range(head_n):
        o_copy(i).wait()

    for d in step1:
        pl.when(ctx + d <= last)(s1_copy(d).wait_send)
    for j, d in enumerate(step2):
        pl.when(ctx + d <= last)(s2_copy(j).wait_send)

    for dz, dc in order[:1] + order[5:]:
        q_copy(peer(dz, dc), head).wait_send()

    @pl.when(ctx + 2 <= last)
    def _():
        far_keys.wait_send()
        hop1.wait_send()

    pl.when(above + 2 <= last)(hop2.wait_send)


def per_device(ctx_n, head_n, q_rows, key_rows, value_rows, doc_lengths, window_widths, sink_widths):
    rows = key_rows.shape[0]
    chunk = q_rows.shape[0]
    docs = doc_lengths.shape[0]
    span = (WSPAN + 1) * rows
    bf = jnp.bfloat16
    n = SINK_MAX
    dma = pltpu.SemaphoreType.DMA
    return pl.pallas_call(
        functools.partial(kernel, ctx_n, head_n, docs),
        out_shape=pltpu.VMEM((rows, QPG * HD), bf),
        in_specs=[pl.BlockSpec(memory_space=pltpu.HBM)] * 6,
        out_specs=pl.BlockSpec(memory_space=pl.ANY),
        scratch_shapes=[
            pltpu.VMEM((head_n, chunk, QPG * HD), bf),
            pltpu.VMEM((span, HD), bf),
            pltpu.VMEM((span, HD), bf),
            pltpu.VMEM((rows, QPG * HD), bf),
            pltpu.VMEM((2 * chunk, WSPAN * rows + chunk + HD), jnp.float32),
            pltpu.VMEM((2, WSPAN * rows + chunk + HD, chunk), bf),
            pltpu.VMEM((chunk, HD), bf),
            pltpu.VMEM((rows // HD, HD), jnp.int32),
            pltpu.VMEM((HD, HD), bf),
            pltpu.VMEM((HD, HD), bf),
            pltpu.VMEM((2 * n, HD), bf),
            pltpu.VMEM((4, 2 * n, HD), bf),
            pltpu.VMEM((2 * n, HD), jnp.float32),
            pltpu.VMEM((2 * n, HD), bf),
            pltpu.VMEM((3, 2 * n, HD), bf),
            pltpu.VMEM((rows, HD), bf),
            pltpu.VMEM((6, chunk * QPG, 2 * HD), jnp.float32),
            pltpu.VMEM((6, chunk * QPG, HD), jnp.float32),
            pltpu.SMEM(doc_lengths.shape, jnp.int32),
            pltpu.SMEM(window_widths.shape, jnp.int32),
            pltpu.SMEM(sink_widths.shape, jnp.int32),
            dma((3,)),
            dma,
            dma((2,)),
            dma((head_n,)),
            dma((head_n,)),
            dma((3, 2)),
            dma((3, 2)),
            dma((2,)),
            dma,
            dma((4,)),
            dma((4,)),
            dma((3,)),
            dma((3,)),
            dma((head_n,)),
        ],
        compiler_params=pltpu.CompilerParams(
            collective_id=0, has_side_effects=True, vmem_limit_bytes=56 * 2**20
        ),
        cost_estimate=pl.CostEstimate(
            flops=4 * rows * QPG * HD * (WSPAN * rows + 2 * chunk),
            bytes_accessed=2 * (2 * rows * QPG * HD + 2 * rows * HD),
            transcendentals=rows * QPG * (WSPAN * rows + 2 * chunk),
        ),
        name="attention",
    )(*[
        pltpu.with_memory_space_constraint(a, pltpu.HBM)
        for a in (doc_lengths, window_widths, sink_widths, q_rows, key_rows, value_rows)
    ])


def solution(mesh):
    in_specs = (P(("ctx", "head"), None), P("ctx", "head"), P("ctx", "head"), P(), P(), P())
    out_specs = P("ctx", "head")
    return jax.shard_map(
        functools.partial(per_device, mesh.shape["ctx"], mesh.shape["head"]),
        mesh=mesh, in_specs=in_specs, out_specs=out_specs, check_vma=False,
    )
```

```python
import functools

import jax
import jax.numpy as jnp
from jax import lax
from jax.experimental import pallas as pl
from jax.experimental.pallas import tpu as pltpu
from jax.sharding import PartitionSpec as P

HD = 128
QPG = 8
WSPAN = 2
SINK_MAX = 32
MESH = pl.DeviceIdType.MESH
EXP2_SCALE = HD ** (-0.5) * 1.4426950408889634
NT = (((1,), (1,)), ((), ()))
HIDDEN = -1e30


def kernel(
    ctx_n, head_n, docs,
    lengths_hbm, windows_hbm, sinks_hbm, q_hbm, k_hbm, v_hbm, out_hbm,
    qbuf, kbuf, vbuf, obuf, held, bias, ident, first_of, sink_k, sink_v, sink_own, sink_in1, sink_sum, sink_mid, sink_in2,
    relay, acc, tops, lengths, windows, sinks,
    small_local, q_local, kv_local, q_send, q_recv, kv_send, kv_recv, relay_send, relay_recv,
    s1_send, s1_recv, s2_send, s2_recv, o_sem,
):
    ctx = lax.axis_index("ctx")
    head = lax.axis_index("head")
    rows = k_hbm.shape[0]
    chunk = q_hbm.shape[0]
    width = QPG * HD
    near = WSPAN * rows
    z, core, zn = head // 2, head % 2, head_n // 2
    base = ctx * rows

    def back_of(c):
        return lax.rem(c + ctx_n, ctx_n)

    def back(d):
        return back_of(ctx + d)

    step1 = (1, 2, 3, 4)
    stride = 4
    step2 = (4, 8, 12)
    order = [(dz, dc) for dz, dc in ((0, 1), (1, 0), (3, 0), (1, 1), (3, 1), (2, 0), (2, 1))]

    x, y = ctx // stride, ctx % stride
    below = x * stride + lax.rem(y + stride - 1, stride)
    above = x * stride + lax.rem(y + 1, stride)
    two_back = back_of(ctx - 2)
    relay_from = two_back // stride * stride + lax.rem(two_back + stride - 1, stride)
    last = ctx_n - 1

    def peer(dz, dc):
        return lax.rem(z + dz, zn) * 2 + lax.rem(core + dc, 2)

    barrier = pltpu.get_barrier_semaphore()
    def greet(c):
        pl.semaphore_signal(barrier, inc=1, device_id=(c, head), device_id_type=MESH)

    for d in step1 + step2[1:]:
        pl.when(ctx >= d)(functools.partial(greet, back(-d)))
    pl.when(ctx >= 2)(functools.partial(greet, relay_from))
    pl.when(above + 2 <= last)(functools.partial(greet, above))
    to_ctx = jnp.minimum(last - ctx, len(step1)) + sum(jnp.where(ctx + d <= last, 1, 0) for d in step2[1:])
    to_ctx = to_ctx + jnp.where(ctx + 2 <= last, 1, 0) + jnp.where(above + 2 <= last, 1, 0)
    for dz, dc in order:
        pl.semaphore_signal(barrier, inc=1, device_id=(ctx, peer(dz, dc)), device_id_type=MESH)

    own_q = pltpu.make_async_copy(
        q_hbm.at[:, pl.ds(pl.multiple_of(head * width, width), width)], qbuf.at[head], q_local
    )
    own_k = pltpu.make_async_copy(k_hbm, kbuf.at[pl.ds(near, rows)], kv_local.at[0])
    own_v = pltpu.make_async_copy(v_hbm, vbuf.at[pl.ds(near, rows)], kv_local.at[1])
    small = [
        pltpu.make_async_copy(src, dst, small_local.at[j])
        for j, (src, dst) in enumerate(((lengths_hbm, lengths), (windows_hbm, windows), (sinks_hbm, sinks)))
    ]
    for copy in small:
        copy.start()
    own_k.start()
    own_v.start()
    own_q.start()
    for copy in small:
        copy.wait()

    starts = []
    running = jnp.int32(0)
    for d in range(docs):
        starts.append(running)
        running = running + lengths[d]

    def start_of(position):
        found = jnp.int32(-1)
        for s in starts:
            found = jnp.where(position >= s, s, found)
        return found

    window = windows[head]
    sink_width = sinks[head]
    last_doc = {d: start_of(base - d * rows + rows - 1) for d in (0,) + step1}
    doc_before = {d: start_of(base - d * rows) for d in step2}
    doc_a = start_of(base)
    doc_b = start_of(base + rows // 2 - 1)
    doc_b = jnp.where(doc_b > base, doc_b, -1)

    iota_r = lax.broadcasted_iota(jnp.int32, (chunk, HD), 0)
    iota_c = lax.broadcasted_iota(jnp.int32, (chunk, HD), 1)
    ident[...] = jnp.where(iota_r == iota_c, 1.0, 0.0).astype(jnp.bfloat16)
    grid_pos = base + lax.broadcasted_iota(jnp.int32, (rows // HD, HD), 0) * HD + lax.broadcasted_iota(
        jnp.int32, (rows // HD, HD), 1
    )
    found = jnp.zeros((rows // HD, HD), jnp.int32)
    for s in starts:
        found = jnp.where(grid_pos >= s, s, found)
    first_of[...] = found
    @pl.when(ctx == 0)
    def _():
        kbuf[pl.ds(rows, rows), :] = jnp.zeros((rows, HD), jnp.bfloat16)
        vbuf[pl.ds(rows, rows), :] = jnp.zeros((rows, HD), jnp.bfloat16)

    @pl.when(ctx < 2)
    def _():
        kbuf[pl.ds(0, rows), :] = jnp.zeros((rows, HD), jnp.bfloat16)
        vbuf[pl.ds(0, rows), :] = jnp.zeros((rows, HD), jnp.bfloat16)

    sink_k[...] = jnp.zeros_like(sink_k)
    sink_v[...] = jnp.zeros_like(sink_v)

    n = SINK_MAX
    srank = lax.broadcasted_iota(jnp.int32, (HD, chunk), 0)

    def place(s):
        dz = jnp.where(s < 2, 0, jnp.where(s < 6, 1 + 2 * (s % 2), 2))
        dc = jnp.where(s < 2, s, jnp.where(s < 6, s // 2 - 1, s - 6))
        return peer(dz, dc)

    def limits(i):
        t = base + i * chunk + lax.broadcasted_iota(jnp.int32, (1, chunk), 1)
        first = first_of[pl.ds(i, 1), :]
        return t, first, jnp.maximum(first, t - window + 1)

    def set_sink_bias(slot, at, t, first):
        doc = jnp.where(srank < n, doc_a, jnp.where(srank < 2 * n, doc_b, -1))
        r = srank % n
        seen = (r < sink_width) & (doc == first) & (doc + r <= t - window)
        bias[slot, pl.ds(at, HD), :] = jnp.where(seen, 0.0, HIDDEN).astype(jnp.bfloat16)

    def pipeline(lo, hi, reach, row_of, with_sinks, stage, wait_queries, on_the_way=()):
        total = reach + (HD if with_sinks else 0)

        def set_bias(i, slot):
            t, first, low = limits(i)
            kp = base - near + row_of(i) + lax.broadcasted_iota(jnp.int32, (reach, chunk), 0)
            bias[slot, pl.ds(0, reach), :] = jnp.where((kp <= t) & (kp >= low), 0.0, HIDDEN).astype(jnp.bfloat16)
            if with_sinks:
                set_sink_bias(slot, reach, t, first)

        def score(i, slot, h):
            keys = kbuf[pl.ds(row_of(i), reach), :]
            if with_sinks:
                keys = jnp.concatenate([keys, sink_k[...]], axis=0)
            keys = jnp.concatenate([keys, bias[slot, pl.ds(0, total), :]], axis=1)
            unit = ident[...]
            left = jnp.concatenate(
                [jnp.concatenate([qbuf[i, :, a * HD : (a + 1) * HD], unit], axis=1) for a in (h, h + 1)], axis=0
            )
            return lax.dot_general(left, keys, NT, preferred_element_type=jnp.float32)

        def finish(s, i, h, scores):
            vals = vbuf[pl.ds(row_of(i), reach), :]
            if with_sinks:
                vals = jnp.concatenate([vals, sink_v[...]], axis=0)
            vals = jnp.concatenate([vals, jnp.ones((total, HD), jnp.bfloat16)], axis=1)
            span = pl.ds(h * chunk, 2 * chunk)
            top = jnp.max(scores, axis=1, keepdims=True)
            if stage == "last":
                old = tops[s, span, :]
                top = jnp.maximum(old[:, :1], top)
            raw = jnp.exp2(scores * EXP2_SCALE - top * EXP2_SCALE).astype(jnp.bfloat16)
            summed = jnp.dot(raw, vals, preferred_element_type=jnp.float32)
            if stage == "first":
                tops[s, span, :] = jnp.broadcast_to(top, (2 * chunk, HD))
                acc[s, span, :] = summed
                return
            if stage == "last":
                factor = jnp.exp2(old * EXP2_SCALE - jnp.broadcast_to(top * EXP2_SCALE, (2 * chunk, HD)))
                summed = summed + acc[s, span, :] * jnp.concatenate([factor, factor], axis=1)
            result = (summed[:, :HD] / summed[:, HD:]).astype(jnp.bfloat16)
            for a in (0, 1):
                obuf[pl.ds(pl.multiple_of(i * chunk, chunk), chunk), (h + a) * HD : (h + a + 1) * HD] = result[
                    a * chunk : (a + 1) * chunk
                ]

        def wait_for(s):
            if wait_queries:
                i = place(s)
                q_copy(i, i).wait_recv()

        def body(step, carry):
            s = lo + 2 * step
            more = s + 2 < hi
            later = jnp.where(more, s + 2, s + 1)
            for k, action in enumerate(on_the_way):
                pl.when(step == k)(action)
            wait_for(s + 1)
            if hi - lo > 2:
                pl.when(more)(functools.partial(wait_for, s + 2))
            set_bias(place(s + 1), 1)
            tiles = [(s + d, place(s + d), d, h) for d in (0, 1) for h in range(0, QPG, 2)]
            scores = held[:, pl.ds(0, total)]
            for at, (chunk_s, i, slot, h) in enumerate(tiles):
                if at + 1 < len(tiles):
                    ahead = score(tiles[at + 1][1], tiles[at + 1][2], tiles[at + 1][3])
                elif hi - lo > 2:
                    set_bias(place(later), 0)
                    ahead = score(place(later), 0, 0)
                finish(chunk_s, i, h, scores)
                scores = ahead
            if hi - lo > 2:
                held[:, pl.ds(0, total)] = scores
            if stage != "first":
                o_copy(place(s)).start()
                o_copy(place(s + 1)).start()
            return carry

        if lo > 0:
            wait_for(lo)
        set_bias(place(lo), 0)
        held[:, pl.ds(0, total)] = score(place(lo), 0, 0)
        if hi - lo > 2:
            lax.fori_loop(0, (hi - lo) // 2, body, 0)
        else:
            body(0, 0)

    def o_copy(i):
        span = pl.ds(pl.multiple_of(i * chunk, chunk), chunk)
        return pltpu.make_async_copy(obuf.at[span], out_hbm.at[span], o_sem.at[i])

    own_k.wait()
    own_v.wait()
    at = base + lax.broadcasted_iota(jnp.int32, (SINK_MAX, rows), 1)
    rank = lax.broadcasted_iota(jnp.int32, (SINK_MAX, rows), 0)
    pick = jnp.concatenate(
        [jnp.where(at == s + rank, 1.0, 0.0).astype(jnp.bfloat16) for s in (last_doc[0], doc_a, doc_b)], axis=0
    )
    own = jnp.concatenate([kbuf[pl.ds(near, rows), :], vbuf[pl.ds(near, rows), :]], axis=1)
    picked = jnp.dot(pick, own, preferred_element_type=jnp.float32).astype(jnp.bfloat16)
    sink_own[pl.ds(0, n), :] = picked[:n, :HD]
    sink_own[pl.ds(n, n), :] = picked[:n, HD:]
    sink_k[pl.ds(0, n), :] = picked[n : 2 * n, :HD]
    sink_v[pl.ds(0, n), :] = picked[n : 2 * n, HD:]
    sink_k[pl.ds(n, n), :] = picked[2 * n : 3 * n, :HD]
    sink_v[pl.ds(n, n), :] = picked[2 * n : 3 * n, HD:]

    pl.semaphore_wait(barrier, len(order) + to_ctx)

    def q_copy(target, source):
        return pltpu.make_async_remote_copy(
            src_ref=q_hbm.at[:, pl.ds(pl.multiple_of(target * width, width), width)],
            dst_ref=qbuf.at[source],
            send_sem=q_send.at[target],
            recv_sem=q_recv.at[source],
            device_id=(ctx, target),
            device_id_type=MESH,
        )

    cut = 3 * chunk

    def kv_copy(d, which, lo, count, sem):
        src = (k_hbm, v_hbm)[which]
        dst = (kbuf, vbuf)[which]
        return pltpu.make_async_remote_copy(
            src_ref=src.at[pl.ds(lo, count)],
            dst_ref=dst.at[pl.ds(near - d * rows + lo, count)],
            send_sem=kv_send.at[sem, which],
            recv_sem=kv_recv.at[sem, which],
            device_id=(back(d), head),
            device_id_type=MESH,
        )

    def late_rows(which):
        return kv_copy(1, which, cut, rows - cut, 0)

    def early_rows(which):
        return kv_copy(1, which, 0, cut, 2)

    far_keys = kv_copy(2, 0, 0, rows, 1)

    hop1 = pltpu.make_async_remote_copy(
        src_ref=v_hbm, dst_ref=relay, send_sem=relay_send.at[0], recv_sem=relay_recv,
        device_id=(below, head), device_id_type=MESH,
    )
    hop2 = pltpu.make_async_remote_copy(
        src_ref=relay, dst_ref=vbuf.at[pl.ds(0, rows)], send_sem=relay_send.at[1], recv_sem=kv_recv.at[1, 1],
        device_id=(back_of(above + 2), head), device_id_type=MESH,
    )
    def s1_copy(d):
        return pltpu.make_async_remote_copy(
            src_ref=sink_own, dst_ref=sink_in1.at[d - 1], send_sem=s1_send.at[d - 1], recv_sem=s1_recv.at[d - 1],
            device_id=(back(d), head), device_id_type=MESH,
        )

    def s2_copy(j):
        return pltpu.make_async_remote_copy(
            src_ref=sink_mid, dst_ref=sink_in2.at[j], send_sem=s2_send.at[j], recv_sem=s2_recv.at[j],
            device_id=(back(step2[j]), head), device_id_type=MESH,
        )

    @pl.when(ctx < last)
    def _():
        for d in step1:
            pl.when(ctx + d <= last)(s1_copy(d).start)
        for which in (0, 1):
            late_rows(which).start()
        for which in (0, 1):
            early_rows(which).start()

    pl.when(ctx + 2 <= last)(hop1.start)
    for dz, dc in order[:5]:
        q_copy(peer(dz, dc), head).start()

    same = lambda a, b: jnp.full((2 * n, HD), a, jnp.int32) == jnp.full((2 * n, HD), b, jnp.int32)
    sink_sum[pl.ds(0, n), :] = sink_k[pl.ds(0, n), :].astype(jnp.float32)
    sink_sum[pl.ds(n, n), :] = sink_v[pl.ds(0, n), :].astype(jnp.float32)
    for d in step1:

        @pl.when(ctx >= d)
        def _(d=d):
            s1_copy(d).wait_recv()
            take = same(last_doc[d], doc_a)
            if d == stride:
                take = take & (same(doc_before[d], doc_a) == False)
            sink_sum[...] += jnp.where(take, sink_in1[d - 1].astype(jnp.float32), 0.0)

    sink_mid[...] = sink_sum[...].astype(jnp.bfloat16)
    for j, d in enumerate(step2):
        pl.when(ctx + d <= last)(s2_copy(j).start)

    def send_far_keys():
        @pl.when(ctx < last)
        def _():
            for which in (0, 1):
                late_rows(which).wait_send()
                early_rows(which).wait_send()

        pl.when(ctx + 2 <= last)(far_keys.start)

    def send_far_queries():
        for dz, dc in order[1:5]:
            q_copy(peer(dz, dc), head).wait_send()
        for dz, dc in order[5:]:
            q_copy(peer(dz, dc), head).start()

    def at_block(i, blocks):
        return pl.multiple_of(i * chunk + blocks * chunk, chunk)

    def relay_on():
        hop1.wait_recv()
        hop2.start()

    pl.when(above + 2 <= last)(relay_on)

    @pl.when(ctx >= 1)
    def _():
        for which in (0, 1):
            late_rows(which).wait_recv()

    own_q.wait()
    per_shard = rows // chunk
    first_reach = per_shard - cut // chunk
    early, middle = 2, 6
    pipeline(
        0, early, (first_reach + 1) * chunk, lambda i: at_block(i, 2 * per_shard - first_reach), False, "first", True
    )

    @pl.when(ctx >= 1)
    def _():
        for which in (0, 1):
            early_rows(which).wait_recv()

    for j, d in enumerate(step2):

        @pl.when(ctx >= d)
        def _(j=j, d=d):
            s2_copy(j).wait_recv()
            sink_sum[...] += jnp.where(same(doc_before[d], doc_a), sink_in2[j].astype(jnp.float32), 0.0)

    sink_k[pl.ds(0, n), :] = sink_sum[pl.ds(0, n), :].astype(jnp.bfloat16)
    sink_v[pl.ds(0, n), :] = sink_sum[pl.ds(n, n), :].astype(jnp.bfloat16)

    send_far_keys()
    pipeline(
        early, middle, rows + chunk, lambda i: at_block(i, per_shard), True, "first", True,
        (lambda: None, send_far_queries),
    )

    @pl.when(ctx >= 2)
    def _():
        far_keys.wait_recv()
        hop2.wait_recv()

    pipeline(0, early, near - first_reach * chunk, lambda i: at_block(i, 0), True, "last", False)
    pipeline(early, middle, rows, lambda i: at_block(i, 0), False, "last", False)
    pipeline(middle, head_n, near + chunk, lambda i: at_block(i, 0), True, "only", True)
    for i in range(head_n):
        o_copy(i).wait()

    for d in step1:
        pl.when(ctx + d <= last)(s1_copy(d).wait_send)
    for j, d in enumerate(step2):
        pl.when(ctx + d <= last)(s2_copy(j).wait_send)

    for dz, dc in order[:1] + order[5:]:
        q_copy(peer(dz, dc), head).wait_send()

    @pl.when(ctx + 2 <= last)
    def _():
        far_keys.wait_send()
        hop1.wait_send()

    pl.when(above + 2 <= last)(hop2.wait_send)


def per_device(ctx_n, head_n, q_rows, key_rows, value_rows, doc_lengths, window_widths, sink_widths):
    rows = key_rows.shape[0]
    chunk = q_rows.shape[0]
    docs = doc_lengths.shape[0]
    span = (WSPAN + 1) * rows
    bf = jnp.bfloat16
    n = SINK_MAX
    dma = pltpu.SemaphoreType.DMA
    return pl.pallas_call(
        functools.partial(kernel, ctx_n, head_n, docs),
        out_shape=pltpu.VMEM((rows, QPG * HD), bf),
        in_specs=[pl.BlockSpec(memory_space=pltpu.HBM)] * 6,
        out_specs=pl.BlockSpec(memory_space=pl.ANY),
        scratch_shapes=[
            pltpu.VMEM((head_n, chunk, QPG * HD), bf),
            pltpu.VMEM((span, HD), bf),
            pltpu.VMEM((span, HD), bf),
            pltpu.VMEM((rows, QPG * HD), bf),
            pltpu.VMEM((2 * chunk, WSPAN * rows + chunk + HD), jnp.float32),
            pltpu.VMEM((2, WSPAN * rows + chunk + HD, chunk), bf),
            pltpu.VMEM((chunk, HD), bf),
            pltpu.VMEM((rows // HD, HD), jnp.int32),
            pltpu.VMEM((HD, HD), bf),
            pltpu.VMEM((HD, HD), bf),
            pltpu.VMEM((2 * n, HD), bf),
            pltpu.VMEM((4, 2 * n, HD), bf),
            pltpu.VMEM((2 * n, HD), jnp.float32),
            pltpu.VMEM((2 * n, HD), bf),
            pltpu.VMEM((3, 2 * n, HD), bf),
            pltpu.VMEM((rows, HD), bf),
            pltpu.VMEM((6, chunk * QPG, 2 * HD), jnp.float32),
            pltpu.VMEM((6, chunk * QPG, HD), jnp.float32),
            pltpu.SMEM(doc_lengths.shape, jnp.int32),
            pltpu.SMEM(window_widths.shape, jnp.int32),
            pltpu.SMEM(sink_widths.shape, jnp.int32),
            dma((3,)),
            dma,
            dma((2,)),
            dma((head_n,)),
            dma((head_n,)),
            dma((3, 2)),
            dma((3, 2)),
            dma((2,)),
            dma,
            dma((4,)),
            dma((4,)),
            dma((3,)),
            dma((3,)),
            dma((head_n,)),
        ],
        compiler_params=pltpu.CompilerParams(
            collective_id=0, has_side_effects=True, vmem_limit_bytes=56 * 2**20
        ),
        cost_estimate=pl.CostEstimate(
            flops=4 * rows * QPG * HD * (WSPAN * rows + 2 * chunk),
            bytes_accessed=2 * (2 * rows * QPG * HD + 2 * rows * HD),
            transcendentals=rows * QPG * (WSPAN * rows + 2 * chunk),
        ),
        name="attention",
    )(*[
        pltpu.with_memory_space_constraint(a, pltpu.HBM)
        for a in (doc_lengths, window_widths, sink_widths, q_rows, key_rows, value_rows)
    ])


def solution(mesh):
    in_specs = (P(("ctx", "head"), None), P("ctx", "head"), P("ctx", "head"), P(), P(), P())
    out_specs = P("ctx", "head")
    return jax.shard_map(
        functools.partial(per_device, mesh.shape["ctx"], mesh.shape["head"]),
        mesh=mesh, in_specs=in_specs, out_specs=out_specs, check_vma=False,
    )
```

```python
import functools

import jax
import jax.numpy as jnp
from jax import lax
from jax.experimental import pallas as pl
from jax.experimental.pallas import tpu as pltpu
from jax.sharding import PartitionSpec as P

HD = 128
QPG = 8
WSPAN = 2
SINK_MAX = 32
MESH = pl.DeviceIdType.MESH
EXP2_SCALE = HD ** (-0.5) * 1.4426950408889634
NT = (((1,), (1,)), ((), ()))
HIDDEN = -1e30


def kernel(
    ctx_n, head_n, docs,
    lengths_hbm, windows_hbm, sinks_hbm, q_hbm, k_hbm, v_hbm, out_hbm,
    qbuf, kbuf, vbuf, obuf, held, bias, ident, first_of, sink_k, sink_v, sink_own, sink_in1, sink_sum, sink_mid, sink_in2,
    relay, acc, tops, lengths, windows, sinks,
    small_local, q_local, kv_local, q_send, q_recv, kv_send, kv_recv, relay_send, relay_recv,
    s1_send, s1_recv, s2_send, s2_recv, o_sem,
):
    ctx = lax.axis_index("ctx")
    head = lax.axis_index("head")
    rows = k_hbm.shape[0]
    chunk = q_hbm.shape[0]
    width = QPG * HD
    near = WSPAN * rows
    z, core, zn = head // 2, head % 2, head_n // 2
    base = ctx * rows

    def back_of(c):
        return lax.rem(c + ctx_n, ctx_n)

    def back(d):
        return back_of(ctx + d)

    step1 = (1, 2, 3, 4)
    stride = 4
    step2 = (4, 8, 12)
    order = [(dz, dc) for dz, dc in ((0, 1), (1, 0), (3, 0), (1, 1), (3, 1), (2, 0), (2, 1))]

    x, y = ctx // stride, ctx % stride
    below = x * stride + lax.rem(y + stride - 1, stride)
    above = x * stride + lax.rem(y + 1, stride)
    two_back = back_of(ctx - 2)
    relay_from = two_back // stride * stride + lax.rem(two_back + stride - 1, stride)
    last = ctx_n - 1

    def peer(dz, dc):
        return lax.rem(z + dz, zn) * 2 + lax.rem(core + dc, 2)

    barrier = pltpu.get_barrier_semaphore()
    def greet(c):
        pl.semaphore_signal(barrier, inc=1, device_id=(c, head), device_id_type=MESH)

    for d in step1 + step2[1:]:
        pl.when(ctx >= d)(functools.partial(greet, back(-d)))
    pl.when(ctx >= 2)(functools.partial(greet, relay_from))
    pl.when(above + 2 <= last)(functools.partial(greet, above))
    to_ctx = jnp.minimum(last - ctx, len(step1)) + sum(jnp.where(ctx + d <= last, 1, 0) for d in step2[1:])
    to_ctx = to_ctx + jnp.where(ctx + 2 <= last, 1, 0) + jnp.where(above + 2 <= last, 1, 0)
    for dz, dc in order:
        pl.semaphore_signal(barrier, inc=1, device_id=(ctx, peer(dz, dc)), device_id_type=MESH)

    own_q = pltpu.make_async_copy(
        q_hbm.at[:, pl.ds(pl.multiple_of(head * width, width), width)], qbuf.at[head], q_local
    )
    own_k = pltpu.make_async_copy(k_hbm, kbuf.at[pl.ds(near, rows)], kv_local.at[0])
    own_v = pltpu.make_async_copy(v_hbm, vbuf.at[pl.ds(near, rows)], kv_local.at[1])
    small = [
        pltpu.make_async_copy(src, dst, small_local.at[j])
        for j, (src, dst) in enumerate(((lengths_hbm, lengths), (windows_hbm, windows), (sinks_hbm, sinks)))
    ]
    for copy in small:
        copy.start()
    own_k.start()
    own_v.start()
    own_q.start()
    for copy in small:
        copy.wait()

    starts = []
    running = jnp.int32(0)
    for d in range(docs):
        starts.append(running)
        running = running + lengths[d]

    def start_of(position):
        found = jnp.int32(-1)
        for s in starts:
            found = jnp.where(position >= s, s, found)
        return found

    window = windows[head]
    sink_width = sinks[head]
    last_doc = {d: start_of(base - d * rows + rows - 1) for d in (0,) + step1}
    doc_before = {d: start_of(base - d * rows) for d in step2}
    doc_a = start_of(base)
    doc_b = start_of(base + rows // 2 - 1)
    doc_b = jnp.where(doc_b > base, doc_b, -1)

    iota_r = lax.broadcasted_iota(jnp.int32, (chunk, HD), 0)
    iota_c = lax.broadcasted_iota(jnp.int32, (chunk, HD), 1)
    ident[...] = jnp.where(iota_r == iota_c, 1.0, 0.0).astype(jnp.bfloat16)
    grid_pos = base + lax.broadcasted_iota(jnp.int32, (rows // HD, HD), 0) * HD + lax.broadcasted_iota(
        jnp.int32, (rows // HD, HD), 1
    )
    found = jnp.zeros((rows // HD, HD), jnp.int32)
    for s in starts:
        found = jnp.where(grid_pos >= s, s, found)
    first_of[...] = found
    @pl.when(ctx == 0)
    def _():
        kbuf[pl.ds(rows, rows), :] = jnp.zeros((rows, HD), jnp.bfloat16)
        vbuf[pl.ds(rows, rows), :] = jnp.zeros((rows, HD), jnp.bfloat16)

    @pl.when(ctx < 2)
    def _():
        kbuf[pl.ds(0, rows), :] = jnp.zeros((rows, HD), jnp.bfloat16)
        vbuf[pl.ds(0, rows), :] = jnp.zeros((rows, HD), jnp.bfloat16)

    sink_k[...] = jnp.zeros_like(sink_k)
    sink_v[...] = jnp.zeros_like(sink_v)

    n = SINK_MAX
    srank = lax.broadcasted_iota(jnp.int32, (HD, chunk), 0)

    def place(s):
        dz = jnp.where(s < 2, 0, jnp.where(s < 6, 1 + 2 * (s % 2), 2))
        dc = jnp.where(s < 2, s, jnp.where(s < 6, s // 2 - 1, s - 6))
        return peer(dz, dc)

    def limits(i):
        t = base + i * chunk + lax.broadcasted_iota(jnp.int32, (1, chunk), 1)
        first = first_of[pl.ds(i, 1), :]
        return t, first, jnp.maximum(first, t - window + 1)

    def set_sink_bias(slot, at, t, first):
        doc = jnp.where(srank < n, doc_a, jnp.where(srank < 2 * n, doc_b, -1))
        r = srank % n
        seen = (r < sink_width) & (doc == first) & (doc + r <= t - window)
        bias[slot, pl.ds(at, HD), :] = jnp.where(seen, 0.0, HIDDEN).astype(jnp.bfloat16)

    def pipeline(lo, hi, reach, row_of, with_sinks, stage, wait_queries, on_the_way=()):
        total = reach + (HD if with_sinks else 0)

        def set_bias(i, slot):
            t, first, low = limits(i)
            kp = base - near + row_of(i) + lax.broadcasted_iota(jnp.int32, (reach, chunk), 0)
            bias[slot, pl.ds(0, reach), :] = jnp.where((kp <= t) & (kp >= low), 0.0, HIDDEN).astype(jnp.bfloat16)
            if with_sinks:
                set_sink_bias(slot, reach, t, first)

        def score(i, slot, h):
            keys = kbuf[pl.ds(row_of(i), reach), :]
            if with_sinks:
                keys = jnp.concatenate([keys, sink_k[...]], axis=0)
            keys = jnp.concatenate([keys, bias[slot, pl.ds(0, total), :]], axis=1)
            unit = ident[...]
            left = jnp.concatenate(
                [jnp.concatenate([qbuf[i, :, a * HD : (a + 1) * HD], unit], axis=1) for a in (h, h + 1)], axis=0
            )
            return lax.dot_general(left, keys, NT, preferred_element_type=jnp.float32)

        def finish(s, i, h, scores):
            vals = vbuf[pl.ds(row_of(i), reach), :]
            if with_sinks:
                vals = jnp.concatenate([vals, sink_v[...]], axis=0)
            vals = jnp.concatenate([vals, jnp.ones((total, HD), jnp.bfloat16)], axis=1)
            span = pl.ds(h * chunk, 2 * chunk)
            top = jnp.max(scores, axis=1, keepdims=True)
            if stage == "last":
                old = tops[s, span, :]
                top = jnp.maximum(old[:, :1], top)
            raw = jnp.exp2(scores * EXP2_SCALE - top * EXP2_SCALE).astype(jnp.bfloat16)
            summed = jnp.dot(raw, vals, preferred_element_type=jnp.float32)
            if stage == "first":
                tops[s, span, :] = jnp.broadcast_to(top, (2 * chunk, HD))
                acc[s, span, :] = summed
                return
            if stage == "last":
                factor = jnp.exp2(old * EXP2_SCALE - jnp.broadcast_to(top * EXP2_SCALE, (2 * chunk, HD)))
                summed = summed + acc[s, span, :] * jnp.concatenate([factor, factor], axis=1)
            result = (summed[:, :HD] / summed[:, HD:]).astype(jnp.bfloat16)
            for a in (0, 1):
                obuf[pl.ds(pl.multiple_of(i * chunk, chunk), chunk), (h + a) * HD : (h + a + 1) * HD] = result[
                    a * chunk : (a + 1) * chunk
                ]

        def wait_for(s):
            if wait_queries:
                i = place(s)
                q_copy(i, i).wait_recv()

        def body(step, carry):
            s = lo + 2 * step
            more = s + 2 < hi
            later = jnp.where(more, s + 2, s + 1)
            for k, action in enumerate(on_the_way):
                pl.when(step == k)(action)
            wait_for(s + 1)
            if hi - lo > 2:
                pl.when(more)(functools.partial(wait_for, s + 2))
            set_bias(place(s + 1), 1)
            tiles = [(s + d, place(s + d), d, h) for d in (0, 1) for h in range(0, QPG, 2)]
            scores = held[:, pl.ds(0, total)]
            for at, (chunk_s, i, slot, h) in enumerate(tiles):
                if at + 1 < len(tiles):
                    ahead = score(tiles[at + 1][1], tiles[at + 1][2], tiles[at + 1][3])
                elif hi - lo > 2:
                    set_bias(place(later), 0)
                    ahead = score(place(later), 0, 0)
                finish(chunk_s, i, h, scores)
                scores = ahead
            if hi - lo > 2:
                held[:, pl.ds(0, total)] = scores
            if stage != "first":
                o_copy(place(s)).start()
                o_copy(place(s + 1)).start()
            return carry

        if lo > 0:
            wait_for(lo)
        set_bias(place(lo), 0)
        held[:, pl.ds(0, total)] = score(place(lo), 0, 0)
        if hi - lo > 2:
            lax.fori_loop(0, (hi - lo) // 2, body, 0)
        else:
            body(0, 0)

    def o_copy(i):
        span = pl.ds(pl.multiple_of(i * chunk, chunk), chunk)
        return pltpu.make_async_copy(obuf.at[span], out_hbm.at[span], o_sem.at[i])

    own_k.wait()
    own_v.wait()
    at = base + lax.broadcasted_iota(jnp.int32, (SINK_MAX, rows), 1)
    rank = lax.broadcasted_iota(jnp.int32, (SINK_MAX, rows), 0)
    pick = jnp.concatenate(
        [jnp.where(at == s + rank, 1.0, 0.0).astype(jnp.bfloat16) for s in (last_doc[0], doc_a, doc_b)], axis=0
    )
    own = jnp.concatenate([kbuf[pl.ds(near, rows), :], vbuf[pl.ds(near, rows), :]], axis=1)
    picked = jnp.dot(pick, own, preferred_element_type=jnp.float32).astype(jnp.bfloat16)
    sink_own[pl.ds(0, n), :] = picked[:n, :HD]
    sink_own[pl.ds(n, n), :] = picked[:n, HD:]
    sink_k[pl.ds(0, n), :] = picked[n : 2 * n, :HD]
    sink_v[pl.ds(0, n), :] = picked[n : 2 * n, HD:]
    sink_k[pl.ds(n, n), :] = picked[2 * n : 3 * n, :HD]
    sink_v[pl.ds(n, n), :] = picked[2 * n : 3 * n, HD:]

    pl.semaphore_wait(barrier, len(order) + to_ctx)

    def q_copy(target, source):
        return pltpu.make_async_remote_copy(
            src_ref=q_hbm.at[:, pl.ds(pl.multiple_of(target * width, width), width)],
            dst_ref=qbuf.at[source],
            send_sem=q_send.at[target],
            recv_sem=q_recv.at[source],
            device_id=(ctx, target),
            device_id_type=MESH,
        )

    cut = 5 * chunk

    def kv_copy(d, which, lo, count, sem):
        src = (k_hbm, v_hbm)[which]
        dst = (kbuf, vbuf)[which]
        return pltpu.make_async_remote_copy(
            src_ref=src.at[pl.ds(lo, count)],
            dst_ref=dst.at[pl.ds(near - d * rows + lo, count)],
            send_sem=kv_send.at[sem, which],
            recv_sem=kv_recv.at[sem, which],
            device_id=(back(d), head),
            device_id_type=MESH,
        )

    def late_rows(which):
        return kv_copy(1, which, cut, rows - cut, 0)

    def early_rows(which):
        return kv_copy(1, which, 0, cut, 2)

    far_keys = kv_copy(2, 0, 0, rows, 1)

    hop1 = pltpu.make_async_remote_copy(
        src_ref=v_hbm, dst_ref=relay, send_sem=relay_send.at[0], recv_sem=relay_recv,
        device_id=(below, head), device_id_type=MESH,
    )
    hop2 = pltpu.make_async_remote_copy(
        src_ref=relay, dst_ref=vbuf.at[pl.ds(0, rows)], send_sem=relay_send.at[1], recv_sem=kv_recv.at[1, 1],
        device_id=(back_of(above + 2), head), device_id_type=MESH,
    )
    def s1_copy(d):
        return pltpu.make_async_remote_copy(
            src_ref=sink_own, dst_ref=sink_in1.at[d - 1], send_sem=s1_send.at[d - 1], recv_sem=s1_recv.at[d - 1],
            device_id=(back(d), head), device_id_type=MESH,
        )

    def s2_copy(j):
        return pltpu.make_async_remote_copy(
            src_ref=sink_mid, dst_ref=sink_in2.at[j], send_sem=s2_send.at[j], recv_sem=s2_recv.at[j],
            device_id=(back(step2[j]), head), device_id_type=MESH,
        )

    @pl.when(ctx < last)
    def _():
        for d in step1:
            pl.when(ctx + d <= last)(s1_copy(d).start)
        for which in (0, 1):
            late_rows(which).start()
        for which in (0, 1):
            early_rows(which).start()

    pl.when(ctx + 2 <= last)(hop1.start)
    for dz, dc in order[:5]:
        q_copy(peer(dz, dc), head).start()

    same = lambda a, b: jnp.full((2 * n, HD), a, jnp.int32) == jnp.full((2 * n, HD), b, jnp.int32)
    sink_sum[pl.ds(0, n), :] = sink_k[pl.ds(0, n), :].astype(jnp.float32)
    sink_sum[pl.ds(n, n), :] = sink_v[pl.ds(0, n), :].astype(jnp.float32)
    for d in step1:

        @pl.when(ctx >= d)
        def _(d=d):
            s1_copy(d).wait_recv()
            take = same(last_doc[d], doc_a)
            if d == stride:
                take = take & (same(doc_before[d], doc_a) == False)
            sink_sum[...] += jnp.where(take, sink_in1[d - 1].astype(jnp.float32), 0.0)

    sink_mid[...] = sink_sum[...].astype(jnp.bfloat16)
    for j, d in enumerate(step2):
        pl.when(ctx + d <= last)(s2_copy(j).start)

    def send_far_keys():
        @pl.when(ctx < last)
        def _():
            for which in (0, 1):
                late_rows(which).wait_send()
                early_rows(which).wait_send()

        pl.when(ctx + 2 <= last)(far_keys.start)

    def send_far_queries():
        for dz, dc in order[1:5]:
            q_copy(peer(dz, dc), head).wait_send()
        for dz, dc in order[5:]:
            q_copy(peer(dz, dc), head).start()

    def at_block(i, blocks):
        return pl.multiple_of(i * chunk + blocks * chunk, chunk)

    def relay_on():
        hop1.wait_recv()
        hop2.start()

    pl.when(above + 2 <= last)(relay_on)

    @pl.when(ctx >= 1)
    def _():
        for which in (0, 1):
            late_rows(which).wait_recv()

    own_q.wait()
    per_shard = rows // chunk
    first_reach = per_shard - cut // chunk
    early, middle = 2, 6
    pipeline(
        0, early, (first_reach + 1) * chunk, lambda i: at_block(i, 2 * per_shard - first_reach), False, "first", True
    )

    @pl.when(ctx >= 1)
    def _():
        for which in (0, 1):
            early_rows(which).wait_recv()

    for j, d in enumerate(step2):

        @pl.when(ctx >= d)
        def _(j=j, d=d):
            s2_copy(j).wait_recv()
            sink_sum[...] += jnp.where(same(doc_before[d], doc_a), sink_in2[j].astype(jnp.float32), 0.0)

    sink_k[pl.ds(0, n), :] = sink_sum[pl.ds(0, n), :].astype(jnp.bfloat16)
    sink_v[pl.ds(0, n), :] = sink_sum[pl.ds(n, n), :].astype(jnp.bfloat16)

    send_far_keys()
    pipeline(
        early, middle, rows + chunk, lambda i: at_block(i, per_shard), True, "first", True,
        (lambda: None, send_far_queries),
    )

    @pl.when(ctx >= 2)
    def _():
        far_keys.wait_recv()
        hop2.wait_recv()

    pipeline(0, early, near - first_reach * chunk, lambda i: at_block(i, 0), True, "last", False)
    pipeline(early, middle, rows, lambda i: at_block(i, 0), False, "last", False)
    pipeline(middle, head_n, near + chunk, lambda i: at_block(i, 0), True, "only", True)
    for i in range(head_n):
        o_copy(i).wait()

    for d in step1:
        pl.when(ctx + d <= last)(s1_copy(d).wait_send)
    for j, d in enumerate(step2):
        pl.when(ctx + d <= last)(s2_copy(j).wait_send)

    for dz, dc in order[:1] + order[5:]:
        q_copy(peer(dz, dc), head).wait_send()

    @pl.when(ctx + 2 <= last)
    def _():
        far_keys.wait_send()
        hop1.wait_send()

    pl.when(above + 2 <= last)(hop2.wait_send)


def per_device(ctx_n, head_n, q_rows, key_rows, value_rows, doc_lengths, window_widths, sink_widths):
    rows = key_rows.shape[0]
    chunk = q_rows.shape[0]
    docs = doc_lengths.shape[0]
    span = (WSPAN + 1) * rows
    bf = jnp.bfloat16
    n = SINK_MAX
    dma = pltpu.SemaphoreType.DMA
    return pl.pallas_call(
        functools.partial(kernel, ctx_n, head_n, docs),
        out_shape=pltpu.VMEM((rows, QPG * HD), bf),
        in_specs=[pl.BlockSpec(memory_space=pltpu.HBM)] * 6,
        out_specs=pl.BlockSpec(memory_space=pl.ANY),
        scratch_shapes=[
            pltpu.VMEM((head_n, chunk, QPG * HD), bf),
            pltpu.VMEM((span, HD), bf),
            pltpu.VMEM((span, HD), bf),
            pltpu.VMEM((rows, QPG * HD), bf),
            pltpu.VMEM((2 * chunk, WSPAN * rows + chunk + HD), jnp.float32),
            pltpu.VMEM((2, WSPAN * rows + chunk + HD, chunk), bf),
            pltpu.VMEM((chunk, HD), bf),
            pltpu.VMEM((rows // HD, HD), jnp.int32),
            pltpu.VMEM((HD, HD), bf),
            pltpu.VMEM((HD, HD), bf),
            pltpu.VMEM((2 * n, HD), bf),
            pltpu.VMEM((4, 2 * n, HD), bf),
            pltpu.VMEM((2 * n, HD), jnp.float32),
            pltpu.VMEM((2 * n, HD), bf),
            pltpu.VMEM((3, 2 * n, HD), bf),
            pltpu.VMEM((rows, HD), bf),
            pltpu.VMEM((6, chunk * QPG, 2 * HD), jnp.float32),
            pltpu.VMEM((6, chunk * QPG, HD), jnp.float32),
            pltpu.SMEM(doc_lengths.shape, jnp.int32),
            pltpu.SMEM(window_widths.shape, jnp.int32),
            pltpu.SMEM(sink_widths.shape, jnp.int32),
            dma((3,)),
            dma,
            dma((2,)),
            dma((head_n,)),
            dma((head_n,)),
            dma((3, 2)),
            dma((3, 2)),
            dma((2,)),
            dma,
            dma((4,)),
            dma((4,)),
            dma((3,)),
            dma((3,)),
            dma((head_n,)),
        ],
        compiler_params=pltpu.CompilerParams(
            collective_id=0, has_side_effects=True, vmem_limit_bytes=56 * 2**20
        ),
        cost_estimate=pl.CostEstimate(
            flops=4 * rows * QPG * HD * (WSPAN * rows + 2 * chunk),
            bytes_accessed=2 * (2 * rows * QPG * HD + 2 * rows * HD),
            transcendentals=rows * QPG * (WSPAN * rows + 2 * chunk),
        ),
        name="attention",
    )(*[
        pltpu.with_memory_space_constraint(a, pltpu.HBM)
        for a in (doc_lengths, window_widths, sink_widths, q_rows, key_rows, value_rows)
    ])


def solution(mesh):
    in_specs = (P(("ctx", "head"), None), P("ctx", "head"), P("ctx", "head"), P(), P(), P())
    out_specs = P("ctx", "head")
    return jax.shard_map(
        functools.partial(per_device, mesh.shape["ctx"], mesh.shape["head"]),
        mesh=mesh, in_specs=in_specs, out_specs=out_specs, check_vma=False,
    )
```
